32 devices in a mesh: groups: 2 (over y), tm: 16 (over z, x, core), rows: 1.
Axes of the slice: x: 2, y: 2, z: 4, core: 2. Of those that a mesh axis runs over, the one named last changes fastest.
Arguments:
- queries: bfloat16 [32, 4, 64, 1024], P(('groups', 'tm'), 'rows'), parts along dimension 0, may hold values from -60 to 60
- keys: bfloat16 [32, 4, 64, 256], P(('groups', 'tm'), 'rows'), parts along dimension 0, may hold values from -4 to 4
- values: bfloat16 [32, 4, 64, 256], P(('groups', 'tm'), 'rows'), parts along dimension 0, may hold values from -6 to 6
- grad_out: bfloat16 [32, 4, 64, 1024], P(('groups', 'tm'), 'rows'), parts along dimension 0, may hold values from -12 to 12
- frame_mask: int32 [32, 16], P('groups'), parts along dimension 0, may hold values 0 or 1
- clip_frames: int32 [12], P('groups'), parts along dimension 0, may hold values from 1 to 4, 16 in all
- offsets: int32 [24, 2], replicated, may hold values from -3 to 3, as said below
Outputs:
- grad_queries: float32 [32, 4, 64, 1024], P(('groups', 'tm'), 'rows'), parts along dimension 0
- grad_keys: float32 [32, 4, 64, 256], P(('groups', 'tm'), 'rows'), parts along dimension 0
- grad_values: float32 [32, 4, 64, 256], P(('groups', 'tm'), 'rows'), parts along dimension 0
The draws below stay inside these ranges and needn't reach their ends.
There are 2 independent parts, one for each index of `groups`. The reference program is written for one: setup_inputs(seed, part) draws one part's arguments, and reference() takes and returns one part's arrays. A program takes and returns all parts, laid end to end along the dimension named above; an argument that names none is the same for every part. Nothing has to cross between parts.
Inputs may be any that keep to these rules, and one draw needn't show every extreme that they name: `offsets`: row 0 is (0, 0) and row 1 is (0, 1); the rows are distinct cells of the 7 x 7 neighbourhood. `clip_frames`: the lengths sum to 16; the longest clip has exactly 4 frames.
All inputs are finite; a program needn't handle non-finite values.
Results may differ from the reference program's by a relative error of at most 0.005.
Values may be sent and summed in bfloat16 or wider, within the bound.
A program may use at most 128 MiB of HBM per device.

```python
import math
import jax
import jax.numpy as jnp
import numpy as np
from jax import lax

HQ = 8
HK = 2
HD = 128
COLS = 64
NBR = 24
IMG_ROWS = 4
FRAMES = 16
CLIP_MOST = 4
CLIPS = 6


def key_field(key):
    full_shape = (FRAMES, IMG_ROWS, COLS, HK * HD)
    return jnp.clip(jax.random.normal(jax.random.fold_in(key, 11), full_shape, jnp.float32), -4.0, 4.0)


def draw_keys(key, part):
    return key_field(key).astype(jnp.bfloat16)


def draw_queries(key, part):
    full_shape = (FRAMES, IMG_ROWS, COLS, HQ * HD)
    field = jnp.clip(jax.random.normal(jax.random.fold_in(key, 12), full_shape, jnp.float32), -4.0, 4.0)
    return field.astype(jnp.bfloat16)


def draw_offsets(key, part):
    order = jax.random.permutation(jax.random.fold_in(key, 21), 47).astype(jnp.int32)
    chosen = order[:NBR - 2]
    cells = chosen + 2 * (chosen >= 24).astype(jnp.int32)
    others = jnp.stack([cells // 7 - 3, cells % 7 - 3], axis=1)
    fixed_rows = jnp.array([[0, 0], [0, 1]], jnp.int32)
    return jnp.concatenate([fixed_rows, others.astype(jnp.int32)], axis=0)


def plant(entries, own_key, low, high):
    longest = entries.shape.index(max(entries.shape))
    spots = []
    for shift in (0, 1):
        where = [jax.random.randint(jax.random.fold_in(own_key, axis), (), 0, length) for axis, length in enumerate(entries.shape)]
        where[longest] = (where[longest] + shift) % entries.shape[longest]
        spots.append(tuple(where))
    return entries.at[spots[0]].set(low).at[spots[1]].set(high)


def shard_levels(stream_key, dims, split, least, high):
    def one(axis_at, shards_of):
        steps = jax.random.uniform(jax.random.fold_in(jax.random.fold_in(stream_key, 6), axis_at), (shards_of,), jnp.float32, least / len(split), high / len(split))
        return jnp.repeat(jnp.exp(steps), dims[axis_at] // shards_of).reshape((-1,) + (1,) * (len(dims) - axis_at - 1))

    factor_of = one(*split[0])
    for cut in split[1:]:
        factor_of = factor_of * one(*cut)
    return factor_of


def profile(amount, total, most, skew):
    portions = [(1 << 20) // math.isqrt(grade ** skew) + 1 for grade in range(2, amount + 1)]
    rest, given = total - most - (amount - 1), [1] * (amount - 1)
    while rest > 0:
        free = [i for i in range(amount - 1) if given[i] < most]
        mass, remaining = sum([portions[i] for i in free]), rest
        for i in free:
            extra = min(most - given[i], max(1, remaining * portions[i] // mass), rest)
            given[i] = given[i] + extra
            rest = rest - extra
    return np.array([most] + given)


def ragged(own_key, amount, total, bound, slope):
    if amount == 2:
        one = jax.random.randint(own_key, (), max(1, total - bound), min(bound, total - 1) + 1)
        return jnp.stack([one, total - one])
    sizes = jnp.asarray(profile(amount, total, bound, slope), jnp.int32)
    couples = (amount - 1) // 2
    source_of, taker = sizes[1:1 + 2 * couples:2], sizes[2:2 + 2 * couples:2]
    room = jnp.minimum(source_of - 1, bound - taker)
    moved = jax.random.randint(jax.random.fold_in(own_key, 1), (couples,), 0, 1 << 20) % (room + 1)
    sizes = sizes.at[1:1 + 2 * couples:2].set(source_of - moved).at[2:2 + 2 * couples:2].set(taker + moved)
    return sizes[jax.random.permutation(jax.random.fold_in(own_key, 2), amount)]


def normal_values(own_key, shape, width, reach, cuts=(), held_as=jnp.bfloat16):
    level = shard_levels(own_key, shape, cuts, -0.22, 0.18) if cuts else 1.0
    result = jax.random.normal(own_key, shape, jnp.float32) * width * level
    return jnp.minimum(jnp.maximum(result, -reach), reach).astype(held_as)


def setup_inputs(seed: int = 0, part: int = 0) -> dict:
    seeds = jax.random.split(jax.random.key(seed), 8)
    part_keys = jax.random.split(jax.random.fold_in(seeds[7], part), 8)
    return {
        "queries": draw_queries(jax.random.fold_in(jax.random.fold_in(seeds[7], part), 71), part),
        "keys": draw_keys(jax.random.fold_in(jax.random.fold_in(seeds[7], part), 71), part),
        "values": normal_values(part_keys[2], (FRAMES, IMG_ROWS, COLS, HK * HD), 1.0, 6.0, ((0, 16),)),
        "grad_out": normal_values(part_keys[3], (FRAMES, IMG_ROWS, COLS, HQ * HD), 2.0, 12.0, ((0, 16),)),
        "frame_mask": plant((jax.random.randint(part_keys[4], (FRAMES, FRAMES), 0, 4) < 3).astype(jnp.int32), jax.random.fold_in(part_keys[4], 1), 0, 1),
        "clip_frames": ragged(part_keys[5], CLIPS, FRAMES, CLIP_MOST, 2).astype(jnp.int32),
        "offsets": draw_offsets(jax.random.fold_in(seeds[7], 71), part),
    }


negative_big = -1.0e30


def cycle_positions(clip_frames, frame_ids):
    clip_ends = jnp.cumsum(clip_frames).astype(jnp.int32)
    clip_starts = (clip_ends - clip_frames).astype(jnp.int32)
    is_longest = (clip_frames == CLIP_MOST).astype(jnp.int32)
    first_longest = (is_longest == 1) & (jnp.cumsum(is_longest) == 1)
    rotation = jnp.sum(jnp.where(first_longest, clip_starts, 0)).astype(jnp.int32)
    position = ((frame_ids + 2 + rotation) % FRAMES).astype(jnp.int32)
    return position, clip_ends


def allowed_table(frame_mask, clip_frames):
    frame_ids = jnp.arange(FRAMES).astype(jnp.int32)
    position, clip_ends = cycle_positions(clip_frames, frame_ids)
    clip_of = jnp.sum((position[:, None] >= clip_ends[None, :]).astype(jnp.int32), axis=1)
    lag_ids = jnp.arange(CLIP_MOST).astype(jnp.int32)
    seen = ((frame_ids[:, None] - lag_ids[None, :]) % FRAMES).astype(jnp.int32)
    same_clip = clip_of[seen] == clip_of[:, None]
    causal = position[seen] <= position[:, None]
    kept = (lag_ids[None, :] <= 1) | (frame_mask[frame_ids[:, None], seen] == 1)
    return same_clip & causal & kept, seen


def reference(queries, keys, values, grad_out, frame_mask, clip_frames, offsets):
    group_size = HQ // HK
    scale = HD ** -0.5
    allowed, seen = allowed_table(frame_mask, clip_frames)
    pads = ((0, 0), (3, 3), (3, 3), (0, 0))
    key_pad = jnp.pad(keys, pads)
    value_pad = jnp.pad(values, pads)
    inside = jnp.pad(jnp.ones((IMG_ROWS, COLS), jnp.float32), 3) > 0.5
    zero_index = jnp.zeros((), jnp.int32)

    def one_frame(carry, frame):
        key_acc, value_acc = carry
        query_now = queries[frame].astype(jnp.float32).reshape(IMG_ROWS, COLS, HK, group_size, HD)
        grad_now = grad_out[frame].astype(jnp.float32).reshape(IMG_ROWS, COLS, HK, group_size, HD)
        frame_list = seen[frame]
        frame_live = allowed[frame]
        key_win = key_pad[frame_list]
        value_win = value_pad[frame_list]
        score_list = []
        grad_list = []
        live_list = []
        for index in range(NBR):
            row_shift = (3 + offsets[index, 0]).astype(jnp.int32)
            col_shift = (3 + offsets[index, 1]).astype(jnp.int32)
            starts = (zero_index, row_shift, col_shift, zero_index)
            size_four = (CLIP_MOST, IMG_ROWS, COLS, HK * HD)
            shifted_key = lax.dynamic_slice(key_win, starts, size_four).astype(jnp.float32).reshape(CLIP_MOST, IMG_ROWS, COLS, HK, HD)
            shifted_value = lax.dynamic_slice(value_win, starts, size_four).astype(jnp.float32).reshape(CLIP_MOST, IMG_ROWS, COLS, HK, HD)
            spatial = lax.dynamic_slice(inside, (row_shift, col_shift), (IMG_ROWS, COLS))
            live_list.append(spatial[None] & frame_live[:, None, None])
            score_list.append(jnp.einsum('rcgad,lrcgd->lrcga', query_now, shifted_key) * scale)
            grad_list.append(jnp.einsum('rcgad,lrcgd->lrcga', grad_now, shifted_value))
        scores = jnp.stack(score_list)
        grad_dots = jnp.stack(grad_list)
        lives = jnp.stack(live_list)[..., None, None]
        masked = jnp.where(lives, scores, negative_big)
        top_score = jnp.max(masked, axis=(0, 1))
        total = jnp.sum(jnp.where(lives, jnp.exp(scores - top_score), 0.0), axis=(0, 1))
        log_total = top_score + jnp.log(total)
        probs = jnp.where(lives, jnp.exp(scores - log_total), 0.0)
        delta = jnp.sum(probs * grad_dots, axis=(0, 1))
        probs_low = lax.optimization_barrier(probs.astype(jnp.bfloat16))
        dscore = lax.optimization_barrier((probs * (grad_dots - delta)).astype(jnp.bfloat16))
        query_grad = jnp.zeros((IMG_ROWS, COLS, HK, group_size, HD), jnp.float32)
        for index in range(NBR):
            row_shift = (3 + offsets[index, 0]).astype(jnp.int32)
            col_shift = (3 + offsets[index, 1]).astype(jnp.int32)
            starts = (zero_index, row_shift, col_shift, zero_index)
            size_four = (CLIP_MOST, IMG_ROWS, COLS, HK * HD)
            shifted_key = lax.dynamic_slice(key_win, starts, size_four).astype(jnp.float32).reshape(CLIP_MOST, IMG_ROWS, COLS, HK, HD)
            score_part = dscore[index].astype(jnp.float32)
            prob_part = probs_low[index].astype(jnp.float32)
            query_grad = query_grad + jnp.einsum('lrcga,lrcgd->rcgad', score_part, shifted_key)
            key_part = jnp.einsum('lrcga,rcgad->lrcgd', score_part, query_now) * scale
            value_part = jnp.einsum('lrcga,rcgad->lrcgd', prob_part, grad_now)
            for distance in range(CLIP_MOST):
                target = frame_list[distance].astype(jnp.int32)
                place = (target, row_shift, col_shift, zero_index)
                block_size = (1, IMG_ROWS, COLS, HK * HD)
                old_key = lax.dynamic_slice(key_acc, place, block_size)
                key_acc = lax.dynamic_update_slice(key_acc, old_key + key_part[distance].reshape(block_size), place)
                old_value = lax.dynamic_slice(value_acc, place, block_size)
                value_acc = lax.dynamic_update_slice(value_acc, old_value + value_part[distance].reshape(block_size), place)
        query_out = (query_grad * scale).reshape(IMG_ROWS, COLS, HQ * HD)
        return (key_acc, value_acc), query_out

    start_acc = jnp.zeros((FRAMES, IMG_ROWS + 6, COLS + 6, HK * HD), jnp.float32)
    (key_acc, value_acc), query_grads = lax.scan(one_frame, (start_acc, start_acc), jnp.arange(FRAMES).astype(jnp.int32))
    return query_grads, key_acc[:, 3:-3, 3:-3], value_acc[:, 3:-3, 3:-3]
```

```python
import jax
import jax.numpy as jnp
from jax import lax
from jax.experimental import pallas as pl
from jax.experimental.pallas import tpu as pltpu
from jax.sharding import PartitionSpec as P

HQ = 8
HK = 2
HD = 128


tile_cols = 8
key_span = 14
negative_big = -1e30


def padded_2(cells, sides, width):
    for axis, dim in sides:
        count = lax.axis_size(axis)
        ends = count - 1
        head = lax.slice_in_dim(cells, 0, width, axis=dim)
        tail = lax.slice_in_dim(cells, cells.shape[dim] - width, cells.shape[dim], axis=dim)
        cells = jnp.concatenate(
            [
                lax.ppermute(tail, axis, [(i, (i + 1) % count) for i in range(ends)]),
                cells,
                lax.ppermute(head, axis, [((i + 1) % count, i) for i in range(ends)]),
            ],
            axis=dim,
        )
    return cells


def passed_along(value, axis, steps):
    count = lax.axis_size(axis)
    pairs = [(source, (source + steps) % count) for source in range(count)]
    return lax.ppermute(value, axis, pairs)


def to_tiles(block, group_size):
    band_rows = block.shape[0]
    count_tiles = block.shape[1] // tile_cols
    shaped = block.reshape(band_rows, count_tiles, tile_cols, HK, group_size, HD)
    shaped = shaped.transpose(1, 3, 4, 0, 2, 5)
    return shaped.reshape(count_tiles, HK, group_size, band_rows * tile_cols, HD)


def from_tiles(tiles, band_rows):
    count_tiles = tiles.shape[0]
    group_size = tiles.shape[2]
    shaped = tiles.reshape(count_tiles, HK, group_size, band_rows, tile_cols, HD)
    shaped = shaped.transpose(3, 0, 4, 1, 2, 5)
    return shaped.reshape(1, band_rows, count_tiles * tile_cols, HK * group_size * HD)


def to_windows(extended):
    ext_rows = extended.shape[1]
    total_width = extended.shape[2]
    padded = jnp.pad(extended, ((0, 0), (0, 0), (3, 3), (0, 0)))
    pieces = [
        padded[:, :, column_tile * tile_cols : column_tile * tile_cols + key_span]
        for column_tile in range(total_width // tile_cols)
    ]
    stacked = jnp.stack(pieces, 0)
    stacked = stacked.reshape(len(pieces), 2, ext_rows, key_span, HK, HD)
    stacked = stacked.transpose(1, 0, 4, 2, 3, 5)
    return stacked.reshape(2, len(pieces), HK, ext_rows * key_span, HD)


def from_windows(window_grads, ext_rows, total_width):
    count_tiles = window_grads.shape[1]
    shaped = window_grads.reshape(2, count_tiles, HK, ext_rows, key_span, HD)
    shaped = shaped.transpose(0, 1, 3, 4, 2, 5).reshape(2, count_tiles, ext_rows, key_span, HK * HD)
    summed = jnp.zeros((2, ext_rows, total_width + 6, HK * HD), jnp.float32)
    for column_tile in range(count_tiles):
        first_col = column_tile * tile_cols
        summed = summed.at[:, :, first_col : first_col + key_span].add(shaped[:, column_tile])
    return summed[:, :, 3 : 3 + total_width]


def spatial_live(offsets, band_rows, total_width):
    ext_rows = band_rows + 6
    count_tiles = total_width // tile_cols
    query_row = jnp.repeat(jnp.arange(band_rows), tile_cols)
    query_col = jnp.tile(jnp.arange(tile_cols), band_rows)
    key_row = jnp.repeat(jnp.arange(ext_rows), key_span)
    key_col = jnp.tile(jnp.arange(key_span), ext_rows)
    delta_row = key_row[None, :] - 3 - query_row[:, None]
    delta_col = key_col[None, :] - 3 - query_col[:, None]
    offset_hit = jnp.any(
        (delta_row[None] == offsets[:, 0, None, None])
        & (delta_col[None] == offsets[:, 1, None, None]),
        axis=0,
    )
    band_index = lax.axis_index("rows")
    image_rows = band_rows * lax.axis_size("rows")
    image_row = band_index * band_rows + key_row - 3
    row_inside = (image_row >= 0) & (image_row < image_rows)
    tile_first = jnp.arange(count_tiles) * tile_cols
    image_col = tile_first[:, None] + key_col[None, :] - 3
    col_inside = (image_col >= 0) & (image_col < total_width)
    return offset_hit[None] & row_inside[None, None] & col_inside[:, None, :]


def running_sum(entries):
    places = jnp.arange(entries.shape[0])
    return jnp.sum(jnp.where(places[None, :] <= places[:, None], entries[None, :], 0), axis=1)


def frame_allowed(frame_mask, clip_frames, distance):
    frames = lax.axis_size("tm")
    lags = min(4, frames)
    own_frame = lax.axis_index("tm")
    seen_frame = (own_frame - distance) % frames
    clip_ends = running_sum(clip_frames)
    clip_starts = clip_ends - clip_frames
    is_longest = (clip_frames == lags).astype(jnp.int32)
    first_longest = (is_longest == 1) & (running_sum(is_longest) == 1)
    rotation = jnp.sum(jnp.where(first_longest, clip_starts, 0))
    own_place = (own_frame + 2 + rotation) % frames
    seen_place = (seen_frame + 2 + rotation) % frames
    own_clip = jnp.sum((own_place >= clip_ends).astype(jnp.int32))
    seen_clip = jnp.sum((seen_place >= clip_ends).astype(jnp.int32))
    grid_rows = jnp.arange(frames)[:, None]
    grid_cols = jnp.arange(frames)[None, :]
    picked = jnp.sum(jnp.where((grid_rows == own_frame) & (grid_cols == seen_frame), frame_mask, 0))
    kept = (picked == 1) | (distance <= 1)
    return (own_clip == seen_clip) & (seen_place <= own_place) & kept


def fold_rims(extended_grads, band_rows):
    interior = extended_grads[:, 3 : 3 + band_rows]
    rim_rows = jnp.concatenate([extended_grads[:, :3], extended_grads[:, band_rows + 3 :]], 1)
    haloed = padded_2(rim_rows.astype(jnp.bfloat16), (("rows", 1),), 3).astype(rim_rows.dtype)
    interior = interior.at[:, :3].add(haloed[:, :3])
    return interior.at[:, band_rows - 3 :].add(haloed[:, 9:])


def body(queries, keys, values, grad_out, frame_mask, clip_frames, offsets):
    band_rows = queries.shape[1]
    total_width = queries.shape[2]
    ext_rows = band_rows + 6
    group_size = HQ // HK
    scale = HD ** (-0.5)
    lags = min(4, lax.axis_size("tm"))
    query_tiles = to_tiles(queries[0], group_size)
    grad_tiles = to_tiles(grad_out[0], group_size)
    spatial = spatial_live(offsets, band_rows, total_width)[:, None, None]
    allowed = [frame_allowed(frame_mask, clip_frames, distance) for distance in range(lags)]
    stacked = jnp.stack([keys[0], values[0]], 0)
    resident = padded_2(stacked, (("rows", 1),), 3)

    def pair_terms(extended):
        windows = to_windows(extended)
        logits = (
            jnp.einsum(
                "cgaqd,cgkd->cgaqk", query_tiles, windows[0], preferred_element_type=jnp.float32
            )
            * scale
        )
        grad_dot = jnp.einsum(
            "cgaqd,cgkd->cgaqk", grad_tiles, windows[1], preferred_element_type=jnp.float32
        )
        return (windows, logits, grad_dot)

    stat_shape = (total_width // tile_cols, HK, group_size, band_rows * tile_cols)
    running = (
        jnp.full(stat_shape, negative_big, jnp.float32),
        jnp.zeros(stat_shape, jnp.float32),
        jnp.zeros(stat_shape, jnp.float32),
    )
    visiting = resident
    visited = []
    for distance in range(lags):
        visited.append(visiting)
        extended = visiting
        live_mask = spatial & allowed[distance]
        run_max, run_sum, run_dot = running
        stat_windows, stat_logits, stat_grad_dot = pair_terms(extended)
        masked = jnp.where(live_mask, stat_logits, negative_big)
        new_max = jnp.maximum(run_max, jnp.max(masked, axis=-1))
        factor = jnp.exp(run_max - new_max)
        weights = jnp.where(live_mask, jnp.exp(stat_logits - new_max[..., None]), 0.0)
        running = (
            new_max,
            run_sum * factor + jnp.sum(weights, axis=-1),
            run_dot * factor + jnp.sum(weights * stat_grad_dot, axis=-1),
        )
        if distance + 1 < lags:
            visiting = passed_along(visiting, "tm", 1)
    log_total = running[0] + jnp.log(running[1])
    mean_grad = running[2] / running[1]
    query_total = jnp.zeros(stat_shape + (HD,), jnp.float32)
    carried = jnp.zeros(resident.shape, jnp.float32)
    visiting = resident
    for distance in range(lags):
        extended = visiting
        live_mask = spatial & allowed[distance]
        grad_windows, grad_logits, grad_grad_dot = pair_terms(extended)
        probs = jnp.where(live_mask, jnp.exp(grad_logits - log_total[..., None]), 0.0)
        probs_low = probs.astype(jnp.bfloat16)
        dscore = (probs * (grad_grad_dot - mean_grad[..., None])).astype(jnp.bfloat16)
        query_part = jnp.einsum(
            "cgaqk,cgkd->cgaqd", dscore, grad_windows[0], preferred_element_type=jnp.float32
        )
        key_part = (
            jnp.einsum("cgaqk,cgaqd->cgkd", dscore, query_tiles, preferred_element_type=jnp.float32)
            * scale
        )
        value_part = jnp.einsum(
            "cgaqk,cgaqd->cgkd", probs_low, grad_tiles, preferred_element_type=jnp.float32
        )
        query_part, window_grads = (query_part, jnp.stack([key_part, value_part], 0))
        query_total = query_total + query_part
        ext_grads = from_windows(window_grads, ext_rows, total_width)
        carried = carried + ext_grads
        if distance + 1 < lags:
            visiting = passed_along(visiting, "tm", 1)
            carried = passed_along(carried, "tm", 1)
    carried = passed_along(carried, "tm", 1 - lags)
    finished = fold_rims(carried, band_rows)
    grad_queries = from_tiles(query_total * scale, band_rows)
    return (grad_queries, finished[0][None], finished[1][None])


MESH = pl.DeviceIdType.MESH
LOG2E = 1.4426950408889634
SCALE = HD**-0.5
GROUP = HQ // HK


def lag_allowed(mask_ref, clip_ref, own_frame, frames, lag):
    clips = clip_ref.shape[0]
    seen_frame = lax.rem(own_frame - lag + frames, frames)
    total = jnp.int32(0)
    rotation = jnp.int32(0)
    found = jnp.int32(0)
    for clip in range(clips):
        length = clip_ref[clip]
        first = jnp.where(length == 4, 1, 0) * (1 - found)
        rotation = rotation + first * total
        found = found + first
        total = total + length
    own_place = own_frame + 2 + rotation
    own_place = jnp.where(own_place >= frames, own_place - frames, own_place)
    own_place = jnp.where(own_place >= frames, own_place - frames, own_place)
    seen_place = seen_frame + 2 + rotation
    seen_place = jnp.where(seen_place >= frames, seen_place - frames, seen_place)
    seen_place = jnp.where(seen_place >= frames, seen_place - frames, seen_place)
    own_clip = jnp.int32(0)
    seen_clip = jnp.int32(0)
    end = jnp.int32(0)
    for clip in range(clips):
        end = end + clip_ref[clip]
        own_clip = own_clip + jnp.where(own_place >= end, 1, 0)
        seen_clip = seen_clip + jnp.where(seen_place >= end, 1, 0)
    kept = jnp.maximum(jnp.where(mask_ref[own_frame, seen_frame] == 1, 1, 0), jnp.where(lag <= 1, 1, 0))
    same = jnp.where(own_clip == seen_clip, 1, 0)
    causal = jnp.where(seen_place <= own_place, 1, 0)
    return kept * same * causal


def fused(
    width, frames,
    mask_ref, clip_ref, offset_ref, query_ref, key_ref, value_ref, cot_ref,
    dq_ref, dk_ref, dv_ref,
    kv, grads, arrived, bias, probs, dots, tops, sums, means, dq_acc, send_sem, recv_sem,
):
    tokens = query_ref.shape[0]
    heads_wide = HK * HD
    own = lax.axis_index("tm")
    core = lax.rem(own, 2)

    def device(step):
        return {"tm": lax.rem(own + step + frames, frames)}

    partner = device(1 - 2 * core)
    ahead, behind = device(2), device(frames - 2)
    far = device(jnp.where(core == 0, frames - 3, 3))
    second_to = device(jnp.where(core == 0, 1, 3))
    second_back = device(jnp.where(core == 0, frames - 3, frames - 1))

    barrier = pltpu.get_barrier_semaphore()
    for peer in (partner, ahead, behind, far):
        pl.semaphore_signal(barrier, inc=1, device_id=peer, device_id_type=MESH)
    kv[0, :, :heads_wide] = key_ref[...]
    kv[0, :, heads_wide:] = value_ref[...]
    pl.semaphore_wait(barrier, 4)

    def remote(index, source, target, peer):
        return pltpu.make_async_remote_copy(
            src_ref=source, dst_ref=target, send_sem=send_sem.at[index], recv_sem=recv_sem.at[index],
            device_id=peer, device_id_type=MESH,
        )

    send_two = remote(0, kv.at[0], kv.at[2], ahead)
    send_one = remote(1, kv.at[0], kv.at[1], second_to)
    relay = remote(2, kv.at[2], kv.at[3], partner)
    send_two.start()
    send_one.start()

    key_id = lax.broadcasted_iota(jnp.int32, (tokens, tokens), 0)
    query_id = lax.broadcasted_iota(jnp.int32, (tokens, tokens), 1)
    delta_col = lax.rem(key_id, width) - lax.rem(query_id, width)
    delta_row = key_id // width - query_id // width
    code = jnp.where((delta_col >= -3) & (delta_col <= 3), delta_row * 8 + delta_col, 1000)

    def mark(index, hit):
        wanted = offset_ref[index, 0] * 8 + offset_ref[index, 1]
        return jnp.where(code == wanted, 0.0, hit)

    bias[...] = lax.fori_loop(
        0, offset_ref.shape[0], mark, jnp.full((tokens, tokens), negative_big, jnp.float32), unroll=True
    )

    def lanes(index):
        return pl.ds(pl.multiple_of(index * HD, HD), HD)

    def scores(role, lag):
        allow = lag_allowed(mask_ref, clip_ref, own, frames, lag)
        shut = jnp.where(allow == 1, 0.0, negative_big).astype(jnp.float32)

        def head(h, _):
            group = h // GROUP
            key = kv[role, :, lanes(group)]
            value = kv[role, :, lanes(HK + group)]
            logit = lax.dot_general(
                key, query_ref[:, lanes(h)], (((1,), (1,)), ((), ())), preferred_element_type=jnp.float32
            )
            dot = lax.dot_general(
                value, cot_ref[:, lanes(h)], (((1,), (1,)), ((), ())), preferred_element_type=jnp.float32
            )
            logit = logit * (SCALE * LOG2E) + (bias[...] + shut)
            top = jnp.max(logit, axis=0, keepdims=True)
            weight = jnp.exp2(logit - top)
            probs[role, h] = weight
            dots[role, h] = dot
            tops[role, h] = top
            sums[role, h] = jnp.sum(weight, axis=0, keepdims=True)
            means[role, h] = jnp.sum(weight * dot, axis=0, keepdims=True)
            return 0

        lax.fori_loop(0, HQ, head, 0, unroll=2)

    lag_second = jnp.where(core == 0, 3, 1)
    lag_relay = jnp.where(core == 0, 1, 3)
    scores(0, jnp.int32(0))
    send_two.wait_recv()
    relay.start()
    scores(2, jnp.int32(2))
    send_one.wait_recv()
    scores(1, lag_second)
    relay.wait_recv()
    scores(3, lag_relay)

    def finish(h, _):
        top = jnp.maximum(jnp.maximum(tops[0, h], tops[1, h]), jnp.maximum(tops[2, h], tops[3, h]))
        factors = [jnp.exp2(tops[role, h] - top) for role in range(4)]
        total = sum(factors[role] * sums[role, h] for role in range(4))
        dot = sum(factors[role] * means[role, h] for role in range(4))
        for role in range(4):
            tops[role, h] = factors[role] / total
        means[0, h] = dot / total
        return 0

    lax.fori_loop(0, HQ, finish, 0)

    def gradients(role, first, store):
        def one_group(group, _):
            key_turned = kv[role, :, lanes(group)].T
            key_sum = None
            value_sum = None
            for a in range(GROUP):
                h = group * GROUP + a
                prob = probs[role, h] * tops[role, h]
                score = (prob * (dots[role, h] - means[0, h])).astype(jnp.bfloat16)
                key_part = jnp.dot(score, query_ref[:, lanes(h)], preferred_element_type=jnp.float32)
                value_part = jnp.dot(
                    prob.astype(jnp.bfloat16), cot_ref[:, lanes(h)], preferred_element_type=jnp.float32
                )
                turned = jnp.dot(key_turned, score, preferred_element_type=jnp.float32)
                key_sum = key_part if a == 0 else key_sum + key_part
                value_sum = value_part if a == 0 else value_sum + value_part
                dq_acc[h] = turned if first else dq_acc[h] + turned
            store(group, key_sum * SCALE, value_sum)
            return 0

        lax.fori_loop(0, HK, one_group, 0)

    def store_out(role):
        def store(group, key_sum, value_sum):
            grads[role, :, lanes(group)] = key_sum.astype(jnp.bfloat16)
            grads[role, :, lanes(HK + group)] = value_sum.astype(jnp.bfloat16)

        return store

    back_relay = remote(3, grads.at[2], arrived.at[2], partner)
    back_two = remote(4, grads.at[1], arrived.at[1], behind)
    back_one = remote(5, grads.at[0], arrived.at[0], second_back)
    gradients(3, True, store_out(2))
    back_relay.start()

    def store_two(group, key_sum, value_sum):
        grads[1, :, lanes(group)] = key_sum.astype(jnp.bfloat16)
        grads[1, :, lanes(HK + group)] = value_sum.astype(jnp.bfloat16)

    gradients(2, False, store_two)
    back_relay.wait_recv()
    grads[1] = (grads[1].astype(jnp.float32) + arrived[2].astype(jnp.float32)).astype(jnp.bfloat16)
    back_two.start()
    gradients(1, False, store_out(0))
    back_one.start()

    def store_own(group, key_sum, value_sum):
        dk_ref[:, lanes(group)] = key_sum
        dv_ref[:, lanes(group)] = value_sum

    gradients(0, False, store_own)

    def query_out(h, _):
        dq_ref[:, lanes(h)] = dq_acc[h].T * SCALE
        return 0

    lax.fori_loop(0, HQ, query_out, 0, unroll=2)
    back_two.wait_recv()
    back_one.wait_recv()
    came = arrived[0].astype(jnp.float32) + arrived[1].astype(jnp.float32)
    dk_ref[...] = dk_ref[...] + came[:, :heads_wide]
    dv_ref[...] = dv_ref[...] + came[:, heads_wide:]
    for copy in (send_two, send_one, relay, back_relay, back_two, back_one):
        copy.wait_send()


def fused_body(queries, keys, values, grad_out, frame_mask, clip_frames, offsets):
    _, rows, width, wide = queries.shape
    tokens = rows * width
    narrow = keys.shape[3]
    frames = lax.axis_size("tm")

    def flat(array):
        return array.reshape(tokens, array.shape[3])

    smem = pl.BlockSpec(memory_space=pltpu.SMEM)
    vmem = pl.BlockSpec(memory_space=pltpu.VMEM)

    def kernel(*refs):
        fused(width, frames, *refs)

    dq, dk, dv = pl.pallas_call(
        kernel,
        out_shape=(
            jax.ShapeDtypeStruct((tokens, wide), jnp.float32),
            jax.ShapeDtypeStruct((tokens, narrow), jnp.float32),
            jax.ShapeDtypeStruct((tokens, narrow), jnp.float32),
        ),
        in_specs=[smem] * 3 + [vmem] * 4,
        out_specs=(vmem, vmem, vmem),
        scratch_shapes=[
            pltpu.VMEM((4, tokens, 2 * narrow), jnp.bfloat16),
            pltpu.VMEM((3, tokens, 2 * narrow), jnp.bfloat16),
            pltpu.VMEM((3, tokens, 2 * narrow), jnp.bfloat16),
            pltpu.VMEM((tokens, tokens), jnp.float32),
            pltpu.VMEM((4, HQ, tokens, tokens), jnp.float32),
            pltpu.VMEM((4, HQ, tokens, tokens), jnp.float32),
            pltpu.VMEM((4, HQ, 1, tokens), jnp.float32),
            pltpu.VMEM((4, HQ, 1, tokens), jnp.float32),
            pltpu.VMEM((4, HQ, 1, tokens), jnp.float32),
            pltpu.VMEM((HQ, HD, tokens), jnp.float32),
            pltpu.SemaphoreType.DMA((6,)),
            pltpu.SemaphoreType.DMA((6,)),
        ],
        compiler_params=pltpu.CompilerParams(
            collective_id=0, has_side_effects=True, vmem_limit_bytes=48 * 1024 * 1024
        ),
    )(frame_mask, clip_frames, offsets, flat(queries), flat(keys), flat(values), flat(grad_out))
    shape = (1, rows, width)
    return dq.reshape(shape + (wide,)), dk.reshape(shape + (narrow,)), dv.reshape(shape + (narrow,))


def solution(mesh):
    whole_rows = mesh.shape["rows"] == 1 and mesh.shape["tm"] % 2 == 0 and mesh.shape["tm"] > 6
    return jax.shard_map(
        fused_body if whole_rows else body,
        mesh=mesh,
        in_specs=(
            P(("groups", "tm"), "rows", None, None),
            P(("groups", "tm"), "rows", None, None),
            P(("groups", "tm"), "rows", None, None),
            P(("groups", "tm"), "rows", None, None),
            P("groups", None),
            P("groups"),
            P(),
        ),
        out_specs=(
            P(("groups", "tm"), "rows", None, None),
            P(("groups", "tm"), "rows", None, None),
            P(("groups", "tm"), "rows", None, None),
        ),
        check_vma=False,
    )
```

```python
import jax
import jax.numpy as jnp
from jax import lax
from jax.experimental import pallas as pl
from jax.experimental.pallas import tpu as pltpu
from jax.sharding import PartitionSpec as P

HQ = 8
HK = 2
HD = 128


tile_cols = 8
key_span = 14
negative_big = -1e30


def padded_2(cells, sides, width):
    for axis, dim in sides:
        count = lax.axis_size(axis)
        ends = count - 1
        head = lax.slice_in_dim(cells, 0, width, axis=dim)
        tail = lax.slice_in_dim(cells, cells.shape[dim] - width, cells.shape[dim], axis=dim)
        cells = jnp.concatenate(
            [
                lax.ppermute(tail, axis, [(i, (i + 1) % count) for i in range(ends)]),
                cells,
                lax.ppermute(head, axis, [((i + 1) % count, i) for i in range(ends)]),
            ],
            axis=dim,
        )
    return cells


def passed_along(value, axis, steps):
    count = lax.axis_size(axis)
    pairs = [(source, (source + steps) % count) for source in range(count)]
    return lax.ppermute(value, axis, pairs)


def to_tiles(block, group_size):
    band_rows = block.shape[0]
    count_tiles = block.shape[1] // tile_cols
    shaped = block.reshape(band_rows, count_tiles, tile_cols, HK, group_size, HD)
    shaped = shaped.transpose(1, 3, 4, 0, 2, 5)
    return shaped.reshape(count_tiles, HK, group_size, band_rows * tile_cols, HD)


def from_tiles(tiles, band_rows):
    count_tiles = tiles.shape[0]
    group_size = tiles.shape[2]
    shaped = tiles.reshape(count_tiles, HK, group_size, band_rows, tile_cols, HD)
    shaped = shaped.transpose(3, 0, 4, 1, 2, 5)
    return shaped.reshape(1, band_rows, count_tiles * tile_cols, HK * group_size * HD)


def to_windows(extended):
    ext_rows = extended.shape[1]
    total_width = extended.shape[2]
    padded = jnp.pad(extended, ((0, 0), (0, 0), (3, 3), (0, 0)))
    pieces = [
        padded[:, :, column_tile * tile_cols : column_tile * tile_cols + key_span]
        for column_tile in range(total_width // tile_cols)
    ]
    stacked = jnp.stack(pieces, 0)
    stacked = stacked.reshape(len(pieces), 2, ext_rows, key_span, HK, HD)
    stacked = stacked.transpose(1, 0, 4, 2, 3, 5)
    return stacked.reshape(2, len(pieces), HK, ext_rows * key_span, HD)


def from_windows(window_grads, ext_rows, total_width):
    count_tiles = window_grads.shape[1]
    shaped = window_grads.reshape(2, count_tiles, HK, ext_rows, key_span, HD)
    shaped = shaped.transpose(0, 1, 3, 4, 2, 5).reshape(2, count_tiles, ext_rows, key_span, HK * HD)
    summed = jnp.zeros((2, ext_rows, total_width + 6, HK * HD), jnp.float32)
    for column_tile in range(count_tiles):
        first_col = column_tile * tile_cols
        summed = summed.at[:, :, first_col : first_col + key_span].add(shaped[:, column_tile])
    return summed[:, :, 3 : 3 + total_width]


def spatial_live(offsets, band_rows, total_width):
    ext_rows = band_rows + 6
    count_tiles = total_width // tile_cols
    query_row = jnp.repeat(jnp.arange(band_rows), tile_cols)
    query_col = jnp.tile(jnp.arange(tile_cols), band_rows)
    key_row = jnp.repeat(jnp.arange(ext_rows), key_span)
    key_col = jnp.tile(jnp.arange(key_span), ext_rows)
    delta_row = key_row[None, :] - 3 - query_row[:, None]
    delta_col = key_col[None, :] - 3 - query_col[:, None]
    offset_hit = jnp.any(
        (delta_row[None] == offsets[:, 0, None, None])
        & (delta_col[None] == offsets[:, 1, None, None]),
        axis=0,
    )
    band_index = lax.axis_index("rows")
    image_rows = band_rows * lax.axis_size("rows")
    image_row = band_index * band_rows + key_row - 3
    row_inside = (image_row >= 0) & (image_row < image_rows)
    tile_first = jnp.arange(count_tiles) * tile_cols
    image_col = tile_first[:, None] + key_col[None, :] - 3
    col_inside = (image_col >= 0) & (image_col < total_width)
    return offset_hit[None] & row_inside[None, None] & col_inside[:, None, :]


def running_sum(entries):
    places = jnp.arange(entries.shape[0])
    return jnp.sum(jnp.where(places[None, :] <= places[:, None], entries[None, :], 0), axis=1)


def frame_allowed(frame_mask, clip_frames, distance):
    frames = lax.axis_size("tm")
    lags = min(4, frames)
    own_frame = lax.axis_index("tm")
    seen_frame = (own_frame - distance) % frames
    clip_ends = running_sum(clip_frames)
    clip_starts = clip_ends - clip_frames
    is_longest = (clip_frames == lags).astype(jnp.int32)
    first_longest = (is_longest == 1) & (running_sum(is_longest) == 1)
    rotation = jnp.sum(jnp.where(first_longest, clip_starts, 0))
    own_place = (own_frame + 2 + rotation) % frames
    seen_place = (seen_frame + 2 + rotation) % frames
    own_clip = jnp.sum((own_place >= clip_ends).astype(jnp.int32))
    seen_clip = jnp.sum((seen_place >= clip_ends).astype(jnp.int32))
    grid_rows = jnp.arange(frames)[:, None]
    grid_cols = jnp.arange(frames)[None, :]
    picked = jnp.sum(jnp.where((grid_rows == own_frame) & (grid_cols == seen_frame), frame_mask, 0))
    kept = (picked == 1) | (distance <= 1)
    return (own_clip == seen_clip) & (seen_place <= own_place) & kept


def fold_rims(extended_grads, band_rows):
    interior = extended_grads[:, 3 : 3 + band_rows]
    rim_rows = jnp.concatenate([extended_grads[:, :3], extended_grads[:, band_rows + 3 :]], 1)
    haloed = padded_2(rim_rows.astype(jnp.bfloat16), (("rows", 1),), 3).astype(rim_rows.dtype)
    interior = interior.at[:, :3].add(haloed[:, :3])
    return interior.at[:, band_rows - 3 :].add(haloed[:, 9:])


def body(queries, keys, values, grad_out, frame_mask, clip_frames, offsets):
    band_rows = queries.shape[1]
    total_width = queries.shape[2]
    ext_rows = band_rows + 6
    group_size = HQ // HK
    scale = HD ** (-0.5)
    lags = min(4, lax.axis_size("tm"))
    query_tiles = to_tiles(queries[0], group_size)
    grad_tiles = to_tiles(grad_out[0], group_size)
    spatial = spatial_live(offsets, band_rows, total_width)[:, None, None]
    allowed = [frame_allowed(frame_mask, clip_frames, distance) for distance in range(lags)]
    stacked = jnp.stack([keys[0], values[0]], 0)
    resident = padded_2(stacked, (("rows", 1),), 3)

    def pair_terms(extended):
        windows = to_windows(extended)
        logits = (
            jnp.einsum(
                "cgaqd,cgkd->cgaqk", query_tiles, windows[0], preferred_element_type=jnp.float32
            )
            * scale
        )
        grad_dot = jnp.einsum(
            "cgaqd,cgkd->cgaqk", grad_tiles, windows[1], preferred_element_type=jnp.float32
        )
        return (windows, logits, grad_dot)

    stat_shape = (total_width // tile_cols, HK, group_size, band_rows * tile_cols)
    running = (
        jnp.full(stat_shape, negative_big, jnp.float32),
        jnp.zeros(stat_shape, jnp.float32),
        jnp.zeros(stat_shape, jnp.float32),
    )
    visiting = resident
    visited = []
    for distance in range(lags):
        visited.append(visiting)
        extended = visiting
        live_mask = spatial & allowed[distance]
        run_max, run_sum, run_dot = running
        stat_windows, stat_logits, stat_grad_dot = pair_terms(extended)
        masked = jnp.where(live_mask, stat_logits, negative_big)
        new_max = jnp.maximum(run_max, jnp.max(masked, axis=-1))
        factor = jnp.exp(run_max - new_max)
        weights = jnp.where(live_mask, jnp.exp(stat_logits - new_max[..., None]), 0.0)
        running = (
            new_max,
            run_sum * factor + jnp.sum(weights, axis=-1),
            run_dot * factor + jnp.sum(weights * stat_grad_dot, axis=-1),
        )
        if distance + 1 < lags:
            visiting = passed_along(visiting, "tm", 1)
    log_total = running[0] + jnp.log(running[1])
    mean_grad = running[2] / running[1]
    query_total = jnp.zeros(stat_shape + (HD,), jnp.float32)
    carried = jnp.zeros(resident.shape, jnp.float32)
    visiting = resident
    for distance in range(lags):
        extended = visiting
        live_mask = spatial & allowed[distance]
        grad_windows, grad_logits, grad_grad_dot = pair_terms(extended)
        probs = jnp.where(live_mask, jnp.exp(grad_logits - log_total[..., None]), 0.0)
        probs_low = probs.astype(jnp.bfloat16)
        dscore = (probs * (grad_grad_dot - mean_grad[..., None])).astype(jnp.bfloat16)
        query_part = jnp.einsum(
            "cgaqk,cgkd->cgaqd", dscore, grad_windows[0], preferred_element_type=jnp.float32
        )
        key_part = (
            jnp.einsum("cgaqk,cgaqd->cgkd", dscore, query_tiles, preferred_element_type=jnp.float32)
            * scale
        )
        value_part = jnp.einsum(
            "cgaqk,cgaqd->cgkd", probs_low, grad_tiles, preferred_element_type=jnp.float32
        )
        query_part, window_grads = (query_part, jnp.stack([key_part, value_part], 0))
        query_total = query_total + query_part
        ext_grads = from_windows(window_grads, ext_rows, total_width)
        carried = carried + ext_grads
        if distance + 1 < lags:
            visiting = passed_along(visiting, "tm", 1)
            carried = passed_along(carried, "tm", 1)
    carried = passed_along(carried, "tm", 1 - lags)
    finished = fold_rims(carried, band_rows)
    grad_queries = from_tiles(query_total * scale, band_rows)
    return (grad_queries, finished[0][None], finished[1][None])


MESH = pl.DeviceIdType.MESH
LOG2E = 1.4426950408889634
SCALE = HD**-0.5
GROUP = HQ // HK


def lag_allowed(mask_ref, clip_ref, own_frame, frames, lag):
    clips = clip_ref.shape[0]
    seen_frame = lax.rem(own_frame - lag + frames, frames)
    total = jnp.int32(0)
    rotation = jnp.int32(0)
    found = jnp.int32(0)
    for clip in range(clips):
        length = clip_ref[clip]
        first = jnp.where(length == 4, 1, 0) * (1 - found)
        rotation = rotation + first * total
        found = found + first
        total = total + length
    own_place = own_frame + 2 + rotation
    own_place = jnp.where(own_place >= frames, own_place - frames, own_place)
    own_place = jnp.where(own_place >= frames, own_place - frames, own_place)
    seen_place = seen_frame + 2 + rotation
    seen_place = jnp.where(seen_place >= frames, seen_place - frames, seen_place)
    seen_place = jnp.where(seen_place >= frames, seen_place - frames, seen_place)
    own_clip = jnp.int32(0)
    seen_clip = jnp.int32(0)
    end = jnp.int32(0)
    for clip in range(clips):
        end = end + clip_ref[clip]
        own_clip = own_clip + jnp.where(own_place >= end, 1, 0)
        seen_clip = seen_clip + jnp.where(seen_place >= end, 1, 0)
    kept = jnp.maximum(jnp.where(mask_ref[own_frame, seen_frame] == 1, 1, 0), jnp.where(lag <= 1, 1, 0))
    same = jnp.where(own_clip == seen_clip, 1, 0)
    causal = jnp.where(seen_place <= own_place, 1, 0)
    return kept * same * causal


def fused(
    width, frames,
    mask_hbm, clip_hbm, offset_hbm, query_hbm, key_hbm, value_hbm, cot_hbm,
    dq_ref, dk_ref, dv_ref,
    mask_ref, clip_ref, offset_ref, query_ref, cot_ref, kv, grads, arrived, bias, probs, dots, tops, sums, means, dq_acc, load_sem, send_sem, recv_sem,
):
    tokens = query_ref.shape[0]
    heads_wide = HK * HD
    pairs = (
        (key_hbm, kv.at[0, :, pl.ds(0, heads_wide)]),
        (value_hbm, kv.at[0, :, pl.ds(heads_wide, heads_wide)]),
        (offset_hbm, offset_ref),
        (clip_hbm, clip_ref),
        (mask_hbm, mask_ref),
        (query_hbm, query_ref),
        (cot_hbm, cot_ref),
    )
    loads = [pltpu.make_async_copy(pair[0], pair[1], load_sem.at[i]) for i, pair in enumerate(pairs)]
    for load in loads:
        load.start()
    own = lax.axis_index("tm")
    core = lax.rem(own, 2)

    def device(step):
        return {"tm": lax.rem(own + step + frames, frames)}

    partner = device(1 - 2 * core)
    ahead, behind = device(2), device(frames - 2)
    far = device(jnp.where(core == 0, frames - 3, 3))
    second_to = device(jnp.where(core == 0, 1, 3))
    second_back = device(jnp.where(core == 0, frames - 3, frames - 1))

    barrier = pltpu.get_barrier_semaphore()
    for peer in (partner, ahead, behind, far):
        pl.semaphore_signal(barrier, inc=1, device_id=peer, device_id_type=MESH)
    for load in loads[:2]:
        load.wait()
    pl.semaphore_wait(barrier, 4)

    def remote(index, source, target, peer):
        return pltpu.make_async_remote_copy(
            src_ref=source, dst_ref=target, send_sem=send_sem.at[index], recv_sem=recv_sem.at[index],
            device_id=peer, device_id_type=MESH,
        )

    send_two = remote(0, kv.at[0], kv.at[2], ahead)
    send_one = remote(1, kv.at[0], kv.at[1], second_to)
    relay = remote(2, kv.at[2], kv.at[3], partner)
    send_two.start()
    for load in loads[2:]:
        load.wait()

    key_id = lax.broadcasted_iota(jnp.int32, (tokens, tokens), 0)
    query_id = lax.broadcasted_iota(jnp.int32, (tokens, tokens), 1)
    delta_col = lax.rem(key_id, width) - lax.rem(query_id, width)
    delta_row = key_id // width - query_id // width
    code = jnp.where((delta_col >= -3) & (delta_col <= 3), delta_row * 8 + delta_col, 1000)

    def mark(index, hit):
        wanted = offset_ref[0, index] * 8 + offset_ref[1, index]
        return jnp.where(code == wanted, 0.0, hit)

    bias[...] = lax.fori_loop(
        0, offset_ref.shape[1], mark, jnp.full((tokens, tokens), negative_big, jnp.float32), unroll=True
    )

    def lanes(index):
        return pl.ds(pl.multiple_of(index * HD, HD), HD)

    def scores(role, lag):
        allow = lag_allowed(mask_ref, clip_ref, own, frames, lag)
        shut = jnp.where(allow == 1, 0.0, negative_big).astype(jnp.float32)

        def head(h, _):
            group = h // GROUP
            key = kv[role, :, lanes(group)]
            value = kv[role, :, lanes(HK + group)]
            logit = lax.dot_general(
                key, query_ref[:, lanes(h)], (((1,), (1,)), ((), ())), preferred_element_type=jnp.float32
            )
            dot = lax.dot_general(
                value, cot_ref[:, lanes(h)], (((1,), (1,)), ((), ())), preferred_element_type=jnp.float32
            )
            logit = logit * (SCALE * LOG2E) + (bias[...] + shut)
            top = jnp.max(logit, axis=0, keepdims=True)
            weight = jnp.exp2(logit - top)
            probs[role, h] = weight
            dots[role, h] = dot
            tops[role, h] = top
            sums[role, h] = jnp.sum(weight, axis=0, keepdims=True)
            means[role, h] = jnp.sum(weight * dot, axis=0, keepdims=True)
            return 0

        lax.fori_loop(0, HQ, head, 0, unroll=4)

    lag_second = jnp.where(core == 0, 3, 1)
    lag_relay = jnp.where(core == 0, 1, 3)
    scores(0, jnp.int32(0))
    send_two.wait_send()
    send_one.start()
    send_two.wait_recv()
    relay.start()
    scores(2, jnp.int32(2))
    relay.wait_recv()
    scores(3, lag_relay)
    send_one.wait_recv()
    scores(1, lag_second)

    def finish(h, _):
        top = jnp.maximum(jnp.maximum(tops[0, h], tops[1, h]), jnp.maximum(tops[2, h], tops[3, h]))
        factors = [jnp.exp2(tops[role, h] - top) for role in range(4)]
        total = sum(factors[role] * sums[role, h] for role in range(4))
        dot = sum(factors[role] * means[role, h] for role in range(4))
        for role in range(4):
            tops[role, h] = factors[role] / total
        means[0, h] = dot / total
        return 0

    lax.fori_loop(0, HQ, finish, 0)

    def gradients(role, first, store):
        def one_group(group, _):
            key_turned = kv[role, :, lanes(group)].T
            key_sum = None
            value_sum = None
            for a in range(GROUP):
                h = group * GROUP + a
                prob = probs[role, h] * tops[role, h]
                score = (prob * (dots[role, h] - means[0, h])).astype(jnp.bfloat16)
                key_part = jnp.dot(score, query_ref[:, lanes(h)], preferred_element_type=jnp.float32)
                value_part = jnp.dot(
                    prob.astype(jnp.bfloat16), cot_ref[:, lanes(h)], preferred_element_type=jnp.float32
                )
                turned = jnp.dot(key_turned, score, preferred_element_type=jnp.float32)
                key_sum = key_part if a == 0 else key_sum + key_part
                value_sum = value_part if a == 0 else value_sum + value_part
                dq_acc[h] = turned if first else dq_acc[h] + turned
            store(group, key_sum * SCALE, value_sum)
            return 0

        lax.fori_loop(0, HK, one_group, 0)

    def store_out(role):
        def store(group, key_sum, value_sum):
            grads[role, :, lanes(group)] = key_sum.astype(jnp.bfloat16)
            grads[role, :, lanes(HK + group)] = value_sum.astype(jnp.bfloat16)

        return store

    back_relay = remote(3, grads.at[2], arrived.at[2], partner)
    back_two = remote(4, grads.at[1], arrived.at[1], behind)
    back_one = remote(5, grads.at[0], arrived.at[0], second_back)
    gradients(3, True, store_out(2))
    back_relay.start()
    gradients(1, False, store_out(0))
    back_one.start()

    def store_two(group, key_sum, value_sum):
        grads[1, :, lanes(group)] = key_sum.astype(jnp.bfloat16)
        grads[1, :, lanes(HK + group)] = value_sum.astype(jnp.bfloat16)

    gradients(2, False, store_two)
    back_relay.wait_recv()
    grads[1] = (grads[1].astype(jnp.float32) + arrived[2].astype(jnp.float32)).astype(jnp.bfloat16)
    back_two.start()

    def store_own(group, key_sum, value_sum):
        dk_ref[:, lanes(group)] = key_sum
        dv_ref[:, lanes(group)] = value_sum

    gradients(0, False, store_own)

    def query_out(h, _):
        dq_ref[:, lanes(h)] = dq_acc[h].T * SCALE
        return 0

    lax.fori_loop(0, HQ, query_out, 0, unroll=4)
    back_two.wait_recv()
    back_one.wait_recv()
    came = arrived[0].astype(jnp.float32) + arrived[1].astype(jnp.float32)
    dk_ref[...] = dk_ref[...] + came[:, :heads_wide]
    dv_ref[...] = dv_ref[...] + came[:, heads_wide:]
    for copy in (send_one, relay, back_relay, back_two, back_one):
        copy.wait_send()


def fused_body(queries, keys, values, grad_out, frame_mask, clip_frames, offsets):
    _, rows, width, wide = queries.shape
    tokens = rows * width
    narrow = keys.shape[3]
    frames = lax.axis_size("tm")

    def flat(array):
        return array.reshape(tokens, array.shape[3])

    hbm = pl.BlockSpec(memory_space=pltpu.HBM)
    vmem = pl.BlockSpec(memory_space=pltpu.VMEM)

    def kernel(*refs):
        fused(width, frames, *refs)

    dq, dk, dv = pl.pallas_call(
        kernel,
        out_shape=(
            jax.ShapeDtypeStruct((tokens, wide), jnp.float32),
            jax.ShapeDtypeStruct((tokens, narrow), jnp.float32),
            jax.ShapeDtypeStruct((tokens, narrow), jnp.float32),
        ),
        in_specs=[hbm] * 7,
        out_specs=(vmem, vmem, vmem),
        scratch_shapes=[
            pltpu.SMEM(frame_mask.shape, jnp.int32),
            pltpu.SMEM(clip_frames.shape, jnp.int32),
            pltpu.SMEM(offsets.shape[::-1], jnp.int32),
            pltpu.VMEM((tokens, wide), jnp.bfloat16),
            pltpu.VMEM((tokens, wide), jnp.bfloat16),
            pltpu.VMEM((4, tokens, 2 * narrow), jnp.bfloat16),
            pltpu.VMEM((3, tokens, 2 * narrow), jnp.bfloat16),
            pltpu.VMEM((3, tokens, 2 * narrow), jnp.bfloat16),
            pltpu.VMEM((tokens, tokens), jnp.float32),
            pltpu.VMEM((4, HQ, tokens, tokens), jnp.float32),
            pltpu.VMEM((4, HQ, tokens, tokens), jnp.float32),
            pltpu.VMEM((4, HQ, 1, tokens), jnp.float32),
            pltpu.VMEM((4, HQ, 1, tokens), jnp.float32),
            pltpu.VMEM((4, HQ, 1, tokens), jnp.float32),
            pltpu.VMEM((HQ, HD, tokens), jnp.float32),
            pltpu.SemaphoreType.DMA((7,)),
            pltpu.SemaphoreType.DMA((6,)),
            pltpu.SemaphoreType.DMA((6,)),
        ],
        compiler_params=pltpu.CompilerParams(
            collective_id=0, has_side_effects=True, vmem_limit_bytes=48 * 1024 * 1024
        ),
    )(frame_mask, clip_frames, offsets.T, flat(queries), flat(keys), flat(values), flat(grad_out))
    shape = (1, rows, width)
    return dq.reshape(shape + (wide,)), dk.reshape(shape + (narrow,)), dv.reshape(shape + (narrow,))


def solution(mesh):
    whole_rows = mesh.shape["rows"] == 1 and mesh.shape["tm"] % 2 == 0 and mesh.shape["tm"] > 6
    return jax.shard_map(
        fused_body if whole_rows else body,
        mesh=mesh,
        in_specs=(
            P(("groups", "tm"), "rows", None, None),
            P(("groups", "tm"), "rows", None, None),
            P(("groups", "tm"), "rows", None, None),
            P(("groups", "tm"), "rows", None, None),
            P("groups", None),
            P("groups"),
            P(),
        ),
        out_specs=(
            P(("groups", "tm"), "rows", None, None),
            P(("groups", "tm"), "rows", None, None),
            P(("groups", "tm"), "rows", None, None),
        ),
        check_vma=False,
    )
```

```python
import jax
import jax.numpy as jnp
from jax import lax
from jax.experimental import pallas as pl
from jax.experimental.pallas import tpu as pltpu
from jax.sharding import PartitionSpec as P

HQ = 8
HK = 2
HD = 128


tile_cols = 8
key_span = 14
negative_big = -1e30


def padded_2(cells, sides, width):
    for axis, dim in sides:
        count = lax.axis_size(axis)
        ends = count - 1
        head = lax.slice_in_dim(cells, 0, width, axis=dim)
        tail = lax.slice_in_dim(cells, cells.shape[dim] - width, cells.shape[dim], axis=dim)
        cells = jnp.concatenate(
            [
                lax.ppermute(tail, axis, [(i, (i + 1) % count) for i in range(ends)]),
                cells,
                lax.ppermute(head, axis, [((i + 1) % count, i) for i in range(ends)]),
            ],
            axis=dim,
        )
    return cells


def passed_along(value, axis, steps):
    count = lax.axis_size(axis)
    pairs = [(source, (source + steps) % count) for source in range(count)]
    return lax.ppermute(value, axis, pairs)


def to_tiles(block, group_size):
    band_rows = block.shape[0]
    count_tiles = block.shape[1] // tile_cols
    shaped = block.reshape(band_rows, count_tiles, tile_cols, HK, group_size, HD)
    shaped = shaped.transpose(1, 3, 4, 0, 2, 5)
    return shaped.reshape(count_tiles, HK, group_size, band_rows * tile_cols, HD)


def from_tiles(tiles, band_rows):
    count_tiles = tiles.shape[0]
    group_size = tiles.shape[2]
    shaped = tiles.reshape(count_tiles, HK, group_size, band_rows, tile_cols, HD)
    shaped = shaped.transpose(3, 0, 4, 1, 2, 5)
    return shaped.reshape(1, band_rows, count_tiles * tile_cols, HK * group_size * HD)


def to_windows(extended):
    ext_rows = extended.shape[1]
    total_width = extended.shape[2]
    padded = jnp.pad(extended, ((0, 0), (0, 0), (3, 3), (0, 0)))
    pieces = [
        padded[:, :, column_tile * tile_cols : column_tile * tile_cols + key_span]
        for column_tile in range(total_width // tile_cols)
    ]
    stacked = jnp.stack(pieces, 0)
    stacked = stacked.reshape(len(pieces), 2, ext_rows, key_span, HK, HD)
    stacked = stacked.transpose(1, 0, 4, 2, 3, 5)
    return stacked.reshape(2, len(pieces), HK, ext_rows * key_span, HD)


def from_windows(window_grads, ext_rows, total_width):
    count_tiles = window_grads.shape[1]
    shaped = window_grads.reshape(2, count_tiles, HK, ext_rows, key_span, HD)
    shaped = shaped.transpose(0, 1, 3, 4, 2, 5).reshape(2, count_tiles, ext_rows, key_span, HK * HD)
    summed = jnp.zeros((2, ext_rows, total_width + 6, HK * HD), jnp.float32)
    for column_tile in range(count_tiles):
        first_col = column_tile * tile_cols
        summed = summed.at[:, :, first_col : first_col + key_span].add(shaped[:, column_tile])
    return summed[:, :, 3 : 3 + total_width]


def spatial_live(offsets, band_rows, total_width):
    ext_rows = band_rows + 6
    count_tiles = total_width // tile_cols
    query_row = jnp.repeat(jnp.arange(band_rows), tile_cols)
    query_col = jnp.tile(jnp.arange(tile_cols), band_rows)
    key_row = jnp.repeat(jnp.arange(ext_rows), key_span)
    key_col = jnp.tile(jnp.arange(key_span), ext_rows)
    delta_row = key_row[None, :] - 3 - query_row[:, None]
    delta_col = key_col[None, :] - 3 - query_col[:, None]
    offset_hit = jnp.any(
        (delta_row[None] == offsets[:, 0, None, None])
        & (delta_col[None] == offsets[:, 1, None, None]),
        axis=0,
    )
    band_index = lax.axis_index("rows")
    image_rows = band_rows * lax.axis_size("rows")
    image_row = band_index * band_rows + key_row - 3
    row_inside = (image_row >= 0) & (image_row < image_rows)
    tile_first = jnp.arange(count_tiles) * tile_cols
    image_col = tile_first[:, None] + key_col[None, :] - 3
    col_inside = (image_col >= 0) & (image_col < total_width)
    return offset_hit[None] & row_inside[None, None] & col_inside[:, None, :]


def running_sum(entries):
    places = jnp.arange(entries.shape[0])
    return jnp.sum(jnp.where(places[None, :] <= places[:, None], entries[None, :], 0), axis=1)


def frame_allowed(frame_mask, clip_frames, distance):
    frames = lax.axis_size("tm")
    lags = min(4, frames)
    own_frame = lax.axis_index("tm")
    seen_frame = (own_frame - distance) % frames
    clip_ends = running_sum(clip_frames)
    clip_starts = clip_ends - clip_frames
    is_longest = (clip_frames == lags).astype(jnp.int32)
    first_longest = (is_longest == 1) & (running_sum(is_longest) == 1)
    rotation = jnp.sum(jnp.where(first_longest, clip_starts, 0))
    own_place = (own_frame + 2 + rotation) % frames
    seen_place = (seen_frame + 2 + rotation) % frames
    own_clip = jnp.sum((own_place >= clip_ends).astype(jnp.int32))
    seen_clip = jnp.sum((seen_place >= clip_ends).astype(jnp.int32))
    grid_rows = jnp.arange(frames)[:, None]
    grid_cols = jnp.arange(frames)[None, :]
    picked = jnp.sum(jnp.where((grid_rows == own_frame) & (grid_cols == seen_frame), frame_mask, 0))
    kept = (picked == 1) | (distance <= 1)
    return (own_clip == seen_clip) & (seen_place <= own_place) & kept


def fold_rims(extended_grads, band_rows):
    interior = extended_grads[:, 3 : 3 + band_rows]
    rim_rows = jnp.concatenate([extended_grads[:, :3], extended_grads[:, band_rows + 3 :]], 1)
    haloed = padded_2(rim_rows.astype(jnp.bfloat16), (("rows", 1),), 3).astype(rim_rows.dtype)
    interior = interior.at[:, :3].add(haloed[:, :3])
    return interior.at[:, band_rows - 3 :].add(haloed[:, 9:])


def body(queries, keys, values, grad_out, frame_mask, clip_frames, offsets):
    band_rows = queries.shape[1]
    total_width = queries.shape[2]
    ext_rows = band_rows + 6
    group_size = HQ // HK
    scale = HD ** (-0.5)
    lags = min(4, lax.axis_size("tm"))
    query_tiles = to_tiles(queries[0], group_size)
    grad_tiles = to_tiles(grad_out[0], group_size)
    spatial = spatial_live(offsets, band_rows, total_width)[:, None, None]
    allowed = [frame_allowed(frame_mask, clip_frames, distance) for distance in range(lags)]
    stacked = jnp.stack([keys[0], values[0]], 0)
    resident = padded_2(stacked, (("rows", 1),), 3)

    def pair_terms(extended):
        windows = to_windows(extended)
        logits = (
            jnp.einsum(
                "cgaqd,cgkd->cgaqk", query_tiles, windows[0], preferred_element_type=jnp.float32
            )
            * scale
        )
        grad_dot = jnp.einsum(
            "cgaqd,cgkd->cgaqk", grad_tiles, windows[1], preferred_element_type=jnp.float32
        )
        return (windows, logits, grad_dot)

    stat_shape = (total_width // tile_cols, HK, group_size, band_rows * tile_cols)
    running = (
        jnp.full(stat_shape, negative_big, jnp.float32),
        jnp.zeros(stat_shape, jnp.float32),
        jnp.zeros(stat_shape, jnp.float32),
    )
    visiting = resident
    visited = []
    for distance in range(lags):
        visited.append(visiting)
        extended = visiting
        live_mask = spatial & allowed[distance]
        run_max, run_sum, run_dot = running
        stat_windows, stat_logits, stat_grad_dot = pair_terms(extended)
        masked = jnp.where(live_mask, stat_logits, negative_big)
        new_max = jnp.maximum(run_max, jnp.max(masked, axis=-1))
        factor = jnp.exp(run_max - new_max)
        weights = jnp.where(live_mask, jnp.exp(stat_logits - new_max[..., None]), 0.0)
        running = (
            new_max,
            run_sum * factor + jnp.sum(weights, axis=-1),
            run_dot * factor + jnp.sum(weights * stat_grad_dot, axis=-1),
        )
        if distance + 1 < lags:
            visiting = passed_along(visiting, "tm", 1)
    log_total = running[0] + jnp.log(running[1])
    mean_grad = running[2] / running[1]
    query_total = jnp.zeros(stat_shape + (HD,), jnp.float32)
    carried = jnp.zeros(resident.shape, jnp.float32)
    visiting = resident
    for distance in range(lags):
        extended = visiting
        live_mask = spatial & allowed[distance]
        grad_windows, grad_logits, grad_grad_dot = pair_terms(extended)
        probs = jnp.where(live_mask, jnp.exp(grad_logits - log_total[..., None]), 0.0)
        probs_low = probs.astype(jnp.bfloat16)
        dscore = (probs * (grad_grad_dot - mean_grad[..., None])).astype(jnp.bfloat16)
        query_part = jnp.einsum(
            "cgaqk,cgkd->cgaqd", dscore, grad_windows[0], preferred_element_type=jnp.float32
        )
        key_part = (
            jnp.einsum("cgaqk,cgaqd->cgkd", dscore, query_tiles, preferred_element_type=jnp.float32)
            * scale
        )
        value_part = jnp.einsum(
            "cgaqk,cgaqd->cgkd", probs_low, grad_tiles, preferred_element_type=jnp.float32
        )
        query_part, window_grads = (query_part, jnp.stack([key_part, value_part], 0))
        query_total = query_total + query_part
        ext_grads = from_windows(window_grads, ext_rows, total_width)
        carried = carried + ext_grads
        if distance + 1 < lags:
            visiting = passed_along(visiting, "tm", 1)
            carried = passed_along(carried, "tm", 1)
    carried = passed_along(carried, "tm", 1 - lags)
    finished = fold_rims(carried, band_rows)
    grad_queries = from_tiles(query_total * scale, band_rows)
    return (grad_queries, finished[0][None], finished[1][None])


MESH = pl.DeviceIdType.MESH
LOG2E = 1.4426950408889634
SCALE = HD**-0.5
GROUP = HQ // HK


def lag_allowed(mask_ref, clip_ref, own_frame, frames, lag):
    clips = clip_ref.shape[0]
    seen_frame = lax.rem(own_frame - lag + frames, frames)
    total = jnp.int32(0)
    rotation = jnp.int32(0)
    found = jnp.int32(0)
    for clip in range(clips):
        length = clip_ref[clip]
        first = jnp.where(length == 4, 1, 0) * (1 - found)
        rotation = rotation + first * total
        found = found + first
        total = total + length
    own_place = own_frame + 2 + rotation
    own_place = jnp.where(own_place >= frames, own_place - frames, own_place)
    own_place = jnp.where(own_place >= frames, own_place - frames, own_place)
    seen_place = seen_frame + 2 + rotation
    seen_place = jnp.where(seen_place >= frames, seen_place - frames, seen_place)
    seen_place = jnp.where(seen_place >= frames, seen_place - frames, seen_place)
    own_clip = jnp.int32(0)
    seen_clip = jnp.int32(0)
    end = jnp.int32(0)
    for clip in range(clips):
        end = end + clip_ref[clip]
        own_clip = own_clip + jnp.where(own_place >= end, 1, 0)
        seen_clip = seen_clip + jnp.where(seen_place >= end, 1, 0)
    kept = jnp.maximum(jnp.where(mask_ref[own_frame, seen_frame] == 1, 1, 0), jnp.where(lag <= 1, 1, 0))
    same = jnp.where(own_clip == seen_clip, 1, 0)
    causal = jnp.where(seen_place <= own_place, 1, 0)
    return kept * same * causal


def fused(
    width, frames,
    mask_hbm, clip_hbm, offset_hbm, query_hbm, key_hbm, value_hbm, cot_hbm,
    dq_hbm, dk_ref, dv_ref,
    dq_ref, mask_ref, clip_ref, offset_ref, query_ref, cot_ref, kv, grads, arrived, bias, probs, dots, tops, sums, means, dq_acc, load_sem, send_sem, recv_sem,
):
    tokens = query_ref.shape[0]
    heads_wide = HK * HD
    pairs = (
        (key_hbm, kv.at[0, :, pl.ds(0, heads_wide)]),
        (value_hbm, kv.at[0, :, pl.ds(heads_wide, heads_wide)]),
        (offset_hbm, offset_ref),
        (clip_hbm, clip_ref),
        (mask_hbm, mask_ref),
        (query_hbm, query_ref),
        (cot_hbm, cot_ref),
    )
    loads = [pltpu.make_async_copy(pair[0], pair[1], load_sem.at[i]) for i, pair in enumerate(pairs)]
    for load in loads:
        load.start()
    own = lax.axis_index("tm")
    core = lax.rem(own, 2)

    def device(step):
        return {"tm": lax.rem(own + step + frames, frames)}

    partner = device(1 - 2 * core)
    ahead, behind = device(2), device(frames - 2)
    far = device(jnp.where(core == 0, frames - 3, 3))
    second_to = device(jnp.where(core == 0, 1, 3))
    second_back = device(jnp.where(core == 0, frames - 3, frames - 1))

    barrier = pltpu.get_barrier_semaphore()
    for peer in (partner, ahead, behind, far):
        pl.semaphore_signal(barrier, inc=1, device_id=peer, device_id_type=MESH)
    for load in loads[:2]:
        load.wait()
    pl.semaphore_wait(barrier, 4)

    def remote(index, source, target, peer):
        return pltpu.make_async_remote_copy(
            src_ref=source, dst_ref=target, send_sem=send_sem.at[index], recv_sem=recv_sem.at[index],
            device_id=peer, device_id_type=MESH,
        )

    send_two = remote(0, kv.at[0], kv.at[2], ahead)
    send_one = remote(1, kv.at[0], kv.at[1], second_to)
    relay = remote(2, kv.at[2], kv.at[3], partner)
    send_two.start()
    for load in loads[2:]:
        load.wait()

    key_id = lax.broadcasted_iota(jnp.int32, (tokens, tokens), 0)
    query_id = lax.broadcasted_iota(jnp.int32, (tokens, tokens), 1)
    delta_col = lax.rem(key_id, width) - lax.rem(query_id, width)
    delta_row = key_id // width - query_id // width
    code = jnp.where((delta_col >= -3) & (delta_col <= 3), delta_row * 8 + delta_col, 1000)

    def mark(index, hit):
        wanted = offset_ref[0, index] * 8 + offset_ref[1, index]
        return jnp.where(code == wanted, 0.0, hit)

    bias[...] = lax.fori_loop(
        0, offset_ref.shape[1], mark, jnp.full((tokens, tokens), negative_big, jnp.float32), unroll=True
    )

    def lanes(index):
        return pl.ds(pl.multiple_of(index * HD, HD), HD)

    def scores(role, lag):
        allow = lag_allowed(mask_ref, clip_ref, own, frames, lag)
        shut = jnp.where(allow == 1, 0.0, negative_big).astype(jnp.float32)

        def head(h, _):
            group = h // GROUP
            key = kv[role, :, lanes(group)]
            value = kv[role, :, lanes(HK + group)]
            logit = lax.dot_general(
                key, query_ref[:, lanes(h)], (((1,), (1,)), ((), ())), preferred_element_type=jnp.float32
            )
            dot = lax.dot_general(
                value, cot_ref[:, lanes(h)], (((1,), (1,)), ((), ())), preferred_element_type=jnp.float32
            )
            logit = logit * (SCALE * LOG2E) + (bias[...] + shut)
            top = jnp.max(logit, axis=0, keepdims=True)
            weight = jnp.exp2(logit - top)
            probs[role, h] = weight
            dots[role, h] = dot
            tops[role, h] = top
            sums[role, h] = jnp.sum(weight, axis=0, keepdims=True)
            means[role, h] = jnp.sum(weight * dot, axis=0, keepdims=True)
            return 0

        lax.fori_loop(0, HQ, head, 0, unroll=4)

    lag_second = jnp.where(core == 0, 3, 1)
    lag_relay = jnp.where(core == 0, 1, 3)
    scores(0, jnp.int32(0))
    send_two.wait_send()
    send_one.start()
    send_two.wait_recv()
    relay.start()
    scores(2, jnp.int32(2))
    relay.wait_recv()
    scores(3, lag_relay)
    send_one.wait_recv()
    scores(1, lag_second)

    def finish(h, _):
        top = jnp.maximum(jnp.maximum(tops[0, h], tops[1, h]), jnp.maximum(tops[2, h], tops[3, h]))
        factors = [jnp.exp2(tops[role, h] - top) for role in range(4)]
        total = sum(factors[role] * sums[role, h] for role in range(4))
        dot = sum(factors[role] * means[role, h] for role in range(4))
        for role in range(4):
            tops[role, h] = factors[role] / total
        means[0, h] = dot / total
        return 0

    lax.fori_loop(0, HQ, finish, 0)

    def gradients(role, first, store):
        def one_group(group, _):
            key_turned = kv[role, :, lanes(group)].T
            key_sum = None
            value_sum = None
            for a in range(GROUP):
                h = group * GROUP + a
                prob = probs[role, h] * tops[role, h]
                score = (prob * (dots[role, h] - means[0, h])).astype(jnp.bfloat16)
                key_part = jnp.dot(score, query_ref[:, lanes(h)], preferred_element_type=jnp.float32)
                value_part = jnp.dot(
                    prob.astype(jnp.bfloat16), cot_ref[:, lanes(h)], preferred_element_type=jnp.float32
                )
                turned = jnp.dot(key_turned, score, preferred_element_type=jnp.float32)
                key_sum = key_part if a == 0 else key_sum + key_part
                value_sum = value_part if a == 0 else value_sum + value_part
                dq_acc[h] = turned if first else dq_acc[h] + turned
            store(group, key_sum * SCALE, value_sum)
            return 0

        lax.fori_loop(0, HK, one_group, 0)

    def store_out(role):
        def store(group, key_sum, value_sum):
            grads[role, :, lanes(group)] = key_sum.astype(jnp.bfloat16)
            grads[role, :, lanes(HK + group)] = value_sum.astype(jnp.bfloat16)

        return store

    back_relay = remote(3, grads.at[2], arrived.at[2], partner)
    back_two = remote(4, grads.at[1], arrived.at[1], behind)
    back_one = remote(5, grads.at[0], arrived.at[0], second_back)
    gradients(3, True, store_out(2))
    back_relay.start()
    gradients(1, False, store_out(0))
    back_one.start()

    def store_two(group, key_sum, value_sum):
        grads[1, :, lanes(group)] = key_sum.astype(jnp.bfloat16)
        grads[1, :, lanes(HK + group)] = value_sum.astype(jnp.bfloat16)

    gradients(2, False, store_two)
    back_relay.wait_recv()
    grads[1] = (grads[1].astype(jnp.float32) + arrived[2].astype(jnp.float32)).astype(jnp.bfloat16)
    back_two.start()

    def store_own(group, key_sum, value_sum):
        dk_ref[:, lanes(group)] = key_sum
        dv_ref[:, lanes(group)] = value_sum

    gradients(0, False, store_own)

    def query_out(h, _):
        dq_ref[:, lanes(h)] = dq_acc[h].T * SCALE
        return 0

    lax.fori_loop(0, HQ, query_out, 0, unroll=4)
    store_queries = pltpu.make_async_copy(dq_ref, dq_hbm, load_sem.at[7])
    store_queries.start()
    back_two.wait_recv()
    back_one.wait_recv()
    came = arrived[0].astype(jnp.float32) + arrived[1].astype(jnp.float32)
    dk_ref[...] = dk_ref[...] + came[:, :heads_wide]
    dv_ref[...] = dv_ref[...] + came[:, heads_wide:]
    for copy in (send_one, relay, back_relay, back_two, back_one):
        copy.wait_send()
    store_queries.wait()


def fused_body(queries, keys, values, grad_out, frame_mask, clip_frames, offsets):
    _, rows, width, wide = queries.shape
    tokens = rows * width
    narrow = keys.shape[3]
    frames = lax.axis_size("tm")

    def flat(array):
        return array.reshape(tokens, array.shape[3])

    hbm = pl.BlockSpec(memory_space=pltpu.HBM)
    vmem = pl.BlockSpec(memory_space=pltpu.VMEM)

    def kernel(*refs):
        fused(width, frames, *refs)

    dq, dk, dv = pl.pallas_call(
        kernel,
        out_shape=(
            jax.ShapeDtypeStruct((tokens, wide), jnp.float32),
            jax.ShapeDtypeStruct((tokens, narrow), jnp.float32),
            jax.ShapeDtypeStruct((tokens, narrow), jnp.float32),
        ),
        in_specs=[hbm] * 7,
        out_specs=(hbm, vmem, vmem),
        scratch_shapes=[
            pltpu.VMEM((tokens, wide), jnp.float32),
            pltpu.SMEM(frame_mask.shape, jnp.int32),
            pltpu.SMEM(clip_frames.shape, jnp.int32),
            pltpu.SMEM(offsets.shape[::-1], jnp.int32),
            pltpu.VMEM((tokens, wide), jnp.bfloat16),
            pltpu.VMEM((tokens, wide), jnp.bfloat16),
            pltpu.VMEM((4, tokens, 2 * narrow), jnp.bfloat16),
            pltpu.VMEM((3, tokens, 2 * narrow), jnp.bfloat16),
            pltpu.VMEM((3, tokens, 2 * narrow), jnp.bfloat16),
            pltpu.VMEM((tokens, tokens), jnp.float32),
            pltpu.VMEM((4, HQ, tokens, tokens), jnp.float32),
            pltpu.VMEM((4, HQ, tokens, tokens), jnp.float32),
            pltpu.VMEM((4, HQ, 1, tokens), jnp.float32),
            pltpu.VMEM((4, HQ, 1, tokens), jnp.float32),
            pltpu.VMEM((4, HQ, 1, tokens), jnp.float32),
            pltpu.VMEM((HQ, HD, tokens), jnp.float32),
            pltpu.SemaphoreType.DMA((8,)),
            pltpu.SemaphoreType.DMA((6,)),
            pltpu.SemaphoreType.DMA((6,)),
        ],
        compiler_params=pltpu.CompilerParams(
            collective_id=0, has_side_effects=True, vmem_limit_bytes=63 * 1024 * 1024 - 65536
        ),
    )(frame_mask, clip_frames, offsets.T, flat(queries), flat(keys), flat(values), flat(grad_out))
    shape = (1, rows, width)
    return dq.reshape(shape + (wide,)), dk.reshape(shape + (narrow,)), dv.reshape(shape + (narrow,))


def solution(mesh):
    whole_rows = mesh.shape["rows"] == 1 and mesh.shape["tm"] % 2 == 0 and mesh.shape["tm"] > 6
    return jax.shard_map(
        fused_body if whole_rows else body,
        mesh=mesh,
        in_specs=(
            P(("groups", "tm"), "rows", None, None),
            P(("groups", "tm"), "rows", None, None),
            P(("groups", "tm"), "rows", None, None),
            P(("groups", "tm"), "rows", None, None),
            P("groups", None),
            P("groups"),
            P(),
        ),
        out_specs=(
            P(("groups", "tm"), "rows", None, None),
            P(("groups", "tm"), "rows", None, None),
            P(("groups", "tm"), "rows", None, None),
        ),
        check_vma=False,
    )
```

```python
import jax
import jax.numpy as jnp
from jax import lax
from jax.experimental import pallas as pl
from jax.experimental.pallas import tpu as pltpu
from jax.sharding import PartitionSpec as P

HQ = 8
HK = 2
HD = 128


tile_cols = 8
key_span = 14
negative_big = -1e30


def padded_2(cells, sides, width):
    for axis, dim in sides:
        count = lax.axis_size(axis)
        ends = count - 1
        head = lax.slice_in_dim(cells, 0, width, axis=dim)
        tail = lax.slice_in_dim(cells, cells.shape[dim] - width, cells.shape[dim], axis=dim)
        cells = jnp.concatenate(
            [
                lax.ppermute(tail, axis, [(i, (i + 1) % count) for i in range(ends)]),
                cells,
                lax.ppermute(head, axis, [((i + 1) % count, i) for i in range(ends)]),
            ],
            axis=dim,
        )
    return cells


def passed_along(value, axis, steps):
    count = lax.axis_size(axis)
    pairs = [(source, (source + steps) % count) for source in range(count)]
    return lax.ppermute(value, axis, pairs)


def to_tiles(block, group_size):
    band_rows = block.shape[0]
    count_tiles = block.shape[1] // tile_cols
    shaped = block.reshape(band_rows, count_tiles, tile_cols, HK, group_size, HD)
    shaped = shaped.transpose(1, 3, 4, 0, 2, 5)
    return shaped.reshape(count_tiles, HK, group_size, band_rows * tile_cols, HD)


def from_tiles(tiles, band_rows):
    count_tiles = tiles.shape[0]
    group_size = tiles.shape[2]
    shaped = tiles.reshape(count_tiles, HK, group_size, band_rows, tile_cols, HD)
    shaped = shaped.transpose(3, 0, 4, 1, 2, 5)
    return shaped.reshape(1, band_rows, count_tiles * tile_cols, HK * group_size * HD)


def to_windows(extended):
    ext_rows = extended.shape[1]
    total_width = extended.shape[2]
    padded = jnp.pad(extended, ((0, 0), (0, 0), (3, 3), (0, 0)))
    pieces = [
        padded[:, :, column_tile * tile_cols : column_tile * tile_cols + key_span]
        for column_tile in range(total_width // tile_cols)
    ]
    stacked = jnp.stack(pieces, 0)
    stacked = stacked.reshape(len(pieces), 2, ext_rows, key_span, HK, HD)
    stacked = stacked.transpose(1, 0, 4, 2, 3, 5)
    return stacked.reshape(2, len(pieces), HK, ext_rows * key_span, HD)


def from_windows(window_grads, ext_rows, total_width):
    count_tiles = window_grads.shape[1]
    shaped = window_grads.reshape(2, count_tiles, HK, ext_rows, key_span, HD)
    shaped = shaped.transpose(0, 1, 3, 4, 2, 5).reshape(2, count_tiles, ext_rows, key_span, HK * HD)
    summed = jnp.zeros((2, ext_rows, total_width + 6, HK * HD), jnp.float32)
    for column_tile in range(count_tiles):
        first_col = column_tile * tile_cols
        summed = summed.at[:, :, first_col : first_col + key_span].add(shaped[:, column_tile])
    return summed[:, :, 3 : 3 + total_width]


def spatial_live(offsets, band_rows, total_width):
    ext_rows = band_rows + 6
    count_tiles = total_width // tile_cols
    query_row = jnp.repeat(jnp.arange(band_rows), tile_cols)
    query_col = jnp.tile(jnp.arange(tile_cols), band_rows)
    key_row = jnp.repeat(jnp.arange(ext_rows), key_span)
    key_col = jnp.tile(jnp.arange(key_span), ext_rows)
    delta_row = key_row[None, :] - 3 - query_row[:, None]
    delta_col = key_col[None, :] - 3 - query_col[:, None]
    offset_hit = jnp.any(
        (delta_row[None] == offsets[:, 0, None, None])
        & (delta_col[None] == offsets[:, 1, None, None]),
        axis=0,
    )
    band_index = lax.axis_index("rows")
    image_rows = band_rows * lax.axis_size("rows")
    image_row = band_index * band_rows + key_row - 3
    row_inside = (image_row >= 0) & (image_row < image_rows)
    tile_first = jnp.arange(count_tiles) * tile_cols
    image_col = tile_first[:, None] + key_col[None, :] - 3
    col_inside = (image_col >= 0) & (image_col < total_width)
    return offset_hit[None] & row_inside[None, None] & col_inside[:, None, :]


def running_sum(entries):
    places = jnp.arange(entries.shape[0])
    return jnp.sum(jnp.where(places[None, :] <= places[:, None], entries[None, :], 0), axis=1)


def frame_allowed(frame_mask, clip_frames, distance):
    frames = lax.axis_size("tm")
    lags = min(4, frames)
    own_frame = lax.axis_index("tm")
    seen_frame = (own_frame - distance) % frames
    clip_ends = running_sum(clip_frames)
    clip_starts = clip_ends - clip_frames
    is_longest = (clip_frames == lags).astype(jnp.int32)
    first_longest = (is_longest == 1) & (running_sum(is_longest) == 1)
    rotation = jnp.sum(jnp.where(first_longest, clip_starts, 0))
    own_place = (own_frame + 2 + rotation) % frames
    seen_place = (seen_frame + 2 + rotation) % frames
    own_clip = jnp.sum((own_place >= clip_ends).astype(jnp.int32))
    seen_clip = jnp.sum((seen_place >= clip_ends).astype(jnp.int32))
    grid_rows = jnp.arange(frames)[:, None]
    grid_cols = jnp.arange(frames)[None, :]
    picked = jnp.sum(jnp.where((grid_rows == own_frame) & (grid_cols == seen_frame), frame_mask, 0))
    kept = (picked == 1) | (distance <= 1)
    return (own_clip == seen_clip) & (seen_place <= own_place) & kept


def fold_rims(extended_grads, band_rows):
    interior = extended_grads[:, 3 : 3 + band_rows]
    rim_rows = jnp.concatenate([extended_grads[:, :3], extended_grads[:, band_rows + 3 :]], 1)
    haloed = padded_2(rim_rows.astype(jnp.bfloat16), (("rows", 1),), 3).astype(rim_rows.dtype)
    interior = interior.at[:, :3].add(haloed[:, :3])
    return interior.at[:, band_rows - 3 :].add(haloed[:, 9:])


def body(queries, keys, values, grad_out, frame_mask, clip_frames, offsets):
    band_rows = queries.shape[1]
    total_width = queries.shape[2]
    ext_rows = band_rows + 6
    group_size = HQ // HK
    scale = HD ** (-0.5)
    lags = min(4, lax.axis_size("tm"))
    query_tiles = to_tiles(queries[0], group_size)
    grad_tiles = to_tiles(grad_out[0], group_size)
    spatial = spatial_live(offsets, band_rows, total_width)[:, None, None]
    allowed = [frame_allowed(frame_mask, clip_frames, distance) for distance in range(lags)]
    stacked = jnp.stack([keys[0], values[0]], 0)
    resident = padded_2(stacked, (("rows", 1),), 3)

    def pair_terms(extended):
        windows = to_windows(extended)
        logits = (
            jnp.einsum(
                "cgaqd,cgkd->cgaqk", query_tiles, windows[0], preferred_element_type=jnp.float32
            )
            * scale
        )
        grad_dot = jnp.einsum(
            "cgaqd,cgkd->cgaqk", grad_tiles, windows[1], preferred_element_type=jnp.float32
        )
        return (windows, logits, grad_dot)

    stat_shape = (total_width // tile_cols, HK, group_size, band_rows * tile_cols)
    running = (
        jnp.full(stat_shape, negative_big, jnp.float32),
        jnp.zeros(stat_shape, jnp.float32),
        jnp.zeros(stat_shape, jnp.float32),
    )
    visiting = resident
    visited = []
    for distance in range(lags):
        visited.append(visiting)
        extended = visiting
        live_mask = spatial & allowed[distance]
        run_max, run_sum, run_dot = running
        stat_windows, stat_logits, stat_grad_dot = pair_terms(extended)
        masked = jnp.where(live_mask, stat_logits, negative_big)
        new_max = jnp.maximum(run_max, jnp.max(masked, axis=-1))
        factor = jnp.exp(run_max - new_max)
        weights = jnp.where(live_mask, jnp.exp(stat_logits - new_max[..., None]), 0.0)
        running = (
            new_max,
            run_sum * factor + jnp.sum(weights, axis=-1),
            run_dot * factor + jnp.sum(weights * stat_grad_dot, axis=-1),
        )
        if distance + 1 < lags:
            visiting = passed_along(visiting, "tm", 1)
    log_total = running[0] + jnp.log(running[1])
    mean_grad = running[2] / running[1]
    query_total = jnp.zeros(stat_shape + (HD,), jnp.float32)
    carried = jnp.zeros(resident.shape, jnp.float32)
    visiting = resident
    for distance in range(lags):
        extended = visiting
        live_mask = spatial & allowed[distance]
        grad_windows, grad_logits, grad_grad_dot = pair_terms(extended)
        probs = jnp.where(live_mask, jnp.exp(grad_logits - log_total[..., None]), 0.0)
        probs_low = probs.astype(jnp.bfloat16)
        dscore = (probs * (grad_grad_dot - mean_grad[..., None])).astype(jnp.bfloat16)
        query_part = jnp.einsum(
            "cgaqk,cgkd->cgaqd", dscore, grad_windows[0], preferred_element_type=jnp.float32
        )
        key_part = (
            jnp.einsum("cgaqk,cgaqd->cgkd", dscore, query_tiles, preferred_element_type=jnp.float32)
            * scale
        )
        value_part = jnp.einsum(
            "cgaqk,cgaqd->cgkd", probs_low, grad_tiles, preferred_element_type=jnp.float32
        )
        query_part, window_grads = (query_part, jnp.stack([key_part, value_part], 0))
        query_total = query_total + query_part
        ext_grads = from_windows(window_grads, ext_rows, total_width)
        carried = carried + ext_grads
        if distance + 1 < lags:
            visiting = passed_along(visiting, "tm", 1)
            carried = passed_along(carried, "tm", 1)
    carried = passed_along(carried, "tm", 1 - lags)
    finished = fold_rims(carried, band_rows)
    grad_queries = from_tiles(query_total * scale, band_rows)
    return (grad_queries, finished[0][None], finished[1][None])


MESH = pl.DeviceIdType.MESH
LOG2E = 1.4426950408889634
SCALE = HD**-0.5
GROUP = HQ // HK


def lag_allowed(mask_ref, clip_ref, own_frame, frames, lag):
    clips = clip_ref.shape[0]
    seen_frame = lax.rem(own_frame - lag + frames, frames)
    total = jnp.int32(0)
    rotation = jnp.int32(0)
    found = jnp.int32(0)
    for clip in range(clips):
        length = clip_ref[clip]
        first = jnp.where(length == 4, 1, 0) * (1 - found)
        rotation = rotation + first * total
        found = found + first
        total = total + length
    own_place = own_frame + 2 + rotation
    own_place = jnp.where(own_place >= frames, own_place - frames, own_place)
    own_place = jnp.where(own_place >= frames, own_place - frames, own_place)
    seen_place = seen_frame + 2 + rotation
    seen_place = jnp.where(seen_place >= frames, seen_place - frames, seen_place)
    seen_place = jnp.where(seen_place >= frames, seen_place - frames, seen_place)
    own_clip = jnp.int32(0)
    seen_clip = jnp.int32(0)
    end = jnp.int32(0)
    for clip in range(clips):
        end = end + clip_ref[clip]
        own_clip = own_clip + jnp.where(own_place >= end, 1, 0)
        seen_clip = seen_clip + jnp.where(seen_place >= end, 1, 0)
    kept = jnp.maximum(jnp.where(mask_ref[own_frame, seen_frame] == 1, 1, 0), jnp.where(lag <= 1, 1, 0))
    same = jnp.where(own_clip == seen_clip, 1, 0)
    causal = jnp.where(seen_place <= own_place, 1, 0)
    return kept * same * causal


def fused(
    width, frames,
    mask_hbm, clip_hbm, offset_hbm, query_hbm, key_hbm, value_hbm, cot_hbm,
    dq_hbm, kv_grads_ref,
    dq_ref, mask_ref, clip_ref, offset_ref, query_ref, cot_ref, kv, grads, arrived, bias, probs, dots, tops, sums, means, dq_acc, load_sem, send_sem, recv_sem,
):
    tokens = query_ref.shape[0]
    heads_wide = HK * HD
    pairs = (
        (key_hbm, kv.at[0, :, pl.ds(0, heads_wide)]),
        (value_hbm, kv.at[0, :, pl.ds(heads_wide, heads_wide)]),
        (offset_hbm, offset_ref),
        (clip_hbm, clip_ref),
        (mask_hbm, mask_ref),
        (query_hbm, query_ref),
        (cot_hbm, cot_ref),
    )
    loads = [pltpu.make_async_copy(pair[0], pair[1], load_sem.at[i]) for i, pair in enumerate(pairs)]
    for load in loads:
        load.start()
    own = lax.axis_index("tm")
    core = lax.rem(own, 2)

    def device(step):
        return {"tm": lax.rem(own + step + frames, frames)}

    partner = device(1 - 2 * core)
    ahead, behind = device(2), device(frames - 2)
    far = device(jnp.where(core == 0, frames - 3, 3))
    second_to = device(jnp.where(core == 0, 1, 3))
    second_back = device(jnp.where(core == 0, frames - 3, frames - 1))

    barrier = pltpu.get_barrier_semaphore()
    for peer in (partner, ahead, behind, far):
        pl.semaphore_signal(barrier, inc=1, device_id=peer, device_id_type=MESH)
    for load in loads[:2]:
        load.wait()
    pl.semaphore_wait(barrier, 4)

    def remote(index, source, target, peer):
        return pltpu.make_async_remote_copy(
            src_ref=source, dst_ref=target, send_sem=send_sem.at[index], recv_sem=recv_sem.at[index],
            device_id=peer, device_id_type=MESH,
        )

    send_two = remote(0, kv.at[0], kv.at[2], ahead)
    send_one = remote(1, kv.at[0], kv.at[1], second_to)
    relay = remote(2, kv.at[2], kv.at[3], partner)
    send_two.start()
    for load in loads[2:]:
        load.wait()

    key_id = lax.broadcasted_iota(jnp.int32, (tokens, tokens), 0)
    query_id = lax.broadcasted_iota(jnp.int32, (tokens, tokens), 1)
    delta_col = lax.rem(key_id, width) - lax.rem(query_id, width)
    delta_row = key_id // width - query_id // width
    code = jnp.where((delta_col >= -3) & (delta_col <= 3), delta_row * 8 + delta_col, 1000)

    def mark(index, hit):
        wanted = offset_ref[0, index] * 8 + offset_ref[1, index]
        return jnp.where(code == wanted, 0.0, hit)

    bias[...] = lax.fori_loop(
        0, offset_ref.shape[1], mark, jnp.full((tokens, tokens), negative_big, jnp.float32), unroll=True
    )

    def lanes(index):
        return pl.ds(pl.multiple_of(index * HD, HD), HD)

    def scores(role, lag):
        allow = lag_allowed(mask_ref, clip_ref, own, frames, lag)
        shut = jnp.where(allow == 1, 0.0, negative_big).astype(jnp.float32)

        def head(h, _):
            group = h // GROUP
            key = kv[role, :, lanes(group)]
            value = kv[role, :, lanes(HK + group)]
            logit = lax.dot_general(
                key, query_ref[:, lanes(h)], (((1,), (1,)), ((), ())), preferred_element_type=jnp.float32
            )
            dot = lax.dot_general(
                value, cot_ref[:, lanes(h)], (((1,), (1,)), ((), ())), preferred_element_type=jnp.float32
            )
            logit = logit * (SCALE * LOG2E) + (bias[...] + shut)
            top = jnp.max(logit, axis=0, keepdims=True)
            weight = jnp.exp2(logit - top)
            probs[role, h] = weight
            dots[role, h] = dot
            tops[role, h] = top
            sums[role, h] = jnp.sum(weight, axis=0, keepdims=True)
            means[role, h] = jnp.sum(weight * dot, axis=0, keepdims=True)
            return 0

        lax.fori_loop(0, HQ, head, 0, unroll=4)

    lag_second = jnp.where(core == 0, 3, 1)
    lag_relay = jnp.where(core == 0, 1, 3)
    scores(0, jnp.int32(0))
    send_two.wait_send()
    send_one.start()
    send_two.wait_recv()
    relay.start()
    scores(2, jnp.int32(2))
    relay.wait_recv()
    scores(3, lag_relay)
    send_one.wait_recv()
    scores(1, lag_second)

    def finish(h, _):
        top = jnp.maximum(jnp.maximum(tops[0, h], tops[1, h]), jnp.maximum(tops[2, h], tops[3, h]))
        factors = [jnp.exp2(tops[role, h] - top) for role in range(4)]
        total = sum(factors[role] * sums[role, h] for role in range(4))
        dot = sum(factors[role] * means[role, h] for role in range(4))
        for role in range(4):
            tops[role, h] = factors[role] / total
        means[0, h] = dot / total
        return 0

    lax.fori_loop(0, HQ, finish, 0)

    def gradients(role, first, store):
        def one_group(group, _):
            key_turned = kv[role, :, lanes(group)].T
            key_sum = None
            value_sum = None
            for a in range(GROUP):
                h = group * GROUP + a
                prob = probs[role, h] * tops[role, h]
                score = (prob * (dots[role, h] - means[0, h])).astype(jnp.bfloat16)
                key_part = jnp.dot(score, query_ref[:, lanes(h)], preferred_element_type=jnp.float32)
                value_part = jnp.dot(
                    prob.astype(jnp.bfloat16), cot_ref[:, lanes(h)], preferred_element_type=jnp.float32
                )
                turned = jnp.dot(key_turned, score, preferred_element_type=jnp.float32)
                key_sum = key_part if a == 0 else key_sum + key_part
                value_sum = value_part if a == 0 else value_sum + value_part
                dq_acc[h] = turned if first else dq_acc[h] + turned
            store(group, key_sum * SCALE, value_sum)
            return 0

        lax.fori_loop(0, HK, one_group, 0)

    def store_out(role):
        def store(group, key_sum, value_sum):
            grads[role, :, lanes(group)] = key_sum.astype(jnp.bfloat16)
            grads[role, :, lanes(HK + group)] = value_sum.astype(jnp.bfloat16)

        return store

    back_relay = remote(3, grads.at[2], arrived.at[2], partner)
    back_two = remote(4, grads.at[1], arrived.at[1], behind)
    back_one = remote(5, grads.at[0], arrived.at[0], second_back)
    gradients(3, True, store_out(2))
    back_relay.start()
    gradients(1, False, store_out(0))
    back_one.start()

    def store_two(group, key_sum, value_sum):
        grads[1, :, lanes(group)] = key_sum.astype(jnp.bfloat16)
        grads[1, :, lanes(HK + group)] = value_sum.astype(jnp.bfloat16)

    gradients(2, False, store_two)
    back_relay.wait_recv()
    grads[1] = (grads[1].astype(jnp.float32) + arrived[2].astype(jnp.float32)).astype(jnp.bfloat16)
    back_two.start()

    def store_own(group, key_sum, value_sum):
        kv_grads_ref[0, :, lanes(group)] = key_sum
        kv_grads_ref[1, :, lanes(group)] = value_sum

    gradients(0, False, store_own)

    def query_out(h, _):
        dq_ref[:, lanes(h)] = dq_acc[h].T * SCALE
        return 0

    lax.fori_loop(0, HQ, query_out, 0, unroll=4)
    store_queries = pltpu.make_async_copy(dq_ref, dq_hbm, load_sem.at[7])
    store_queries.start()
    back_two.wait_recv()
    back_one.wait_recv()
    came = arrived[0].astype(jnp.float32) + arrived[1].astype(jnp.float32)
    kv_grads_ref[0] = kv_grads_ref[0] + came[:, :heads_wide]
    kv_grads_ref[1] = kv_grads_ref[1] + came[:, heads_wide:]
    for copy in (send_one, relay, back_relay, back_two, back_one):
        copy.wait_send()
    store_queries.wait()


def fused_body(queries, keys, values, grad_out, frame_mask, clip_frames, offsets):
    _, rows, width, wide = queries.shape
    tokens = rows * width
    narrow = keys.shape[3]
    frames = lax.axis_size("tm")

    def flat(array):
        return array.reshape(tokens, array.shape[3])

    hbm = pl.BlockSpec(memory_space=pltpu.HBM)
    vmem = pl.BlockSpec(memory_space=pltpu.VMEM)

    def kernel(*refs):
        fused(width, frames, *refs)

    dq, kv_grads = pl.pallas_call(
        kernel,
        out_shape=(
            jax.ShapeDtypeStruct((tokens, wide), jnp.float32),
            jax.ShapeDtypeStruct((2, tokens, narrow), jnp.float32),
        ),
        in_specs=[hbm] * 7,
        out_specs=(hbm, vmem),
        scratch_shapes=[
            pltpu.VMEM((tokens, wide), jnp.float32),
            pltpu.SMEM(frame_mask.shape, jnp.int32),
            pltpu.SMEM(clip_frames.shape, jnp.int32),
            pltpu.SMEM(offsets.shape[::-1], jnp.int32),
            pltpu.VMEM((tokens, wide), jnp.bfloat16),
            pltpu.VMEM((tokens, wide), jnp.bfloat16),
            pltpu.VMEM((4, tokens, 2 * narrow), jnp.bfloat16),
            pltpu.VMEM((3, tokens, 2 * narrow), jnp.bfloat16),
            pltpu.VMEM((3, tokens, 2 * narrow), jnp.bfloat16),
            pltpu.VMEM((tokens, tokens), jnp.float32),
            pltpu.VMEM((4, HQ, tokens, tokens), jnp.float32),
            pltpu.VMEM((4, HQ, tokens, tokens), jnp.float32),
            pltpu.VMEM((4, HQ, 1, tokens), jnp.float32),
            pltpu.VMEM((4, HQ, 1, tokens), jnp.float32),
            pltpu.VMEM((4, HQ, 1, tokens), jnp.float32),
            pltpu.VMEM((HQ, HD, tokens), jnp.float32),
            pltpu.SemaphoreType.DMA((8,)),
            pltpu.SemaphoreType.DMA((6,)),
            pltpu.SemaphoreType.DMA((6,)),
        ],
        compiler_params=pltpu.CompilerParams(
            collective_id=0, has_side_effects=True, vmem_limit_bytes=63 * 1024 * 1024 - 65536
        ),
    )(frame_mask, clip_frames, offsets.T, flat(queries), flat(keys), flat(values), flat(grad_out))
    shape = (1, rows, width)
    return dq.reshape(shape + (wide,)), kv_grads[0].reshape(shape + (narrow,)), kv_grads[1].reshape(shape + (narrow,))


def solution(mesh):
    whole_rows = mesh.shape["rows"] == 1 and mesh.shape["tm"] % 2 == 0 and mesh.shape["tm"] > 6
    return jax.shard_map(
        fused_body if whole_rows else body,
        mesh=mesh,
        in_specs=(
            P(("groups", "tm"), "rows", None, None),
            P(("groups", "tm"), "rows", None, None),
            P(("groups", "tm"), "rows", None, None),
            P(("groups", "tm"), "rows", None, None),
            P("groups", None),
            P("groups"),
            P(),
        ),
        out_specs=(
            P(("groups", "tm"), "rows", None, None),
            P(("groups", "tm"), "rows", None, None),
            P(("groups", "tm"), "rows", None, None),
        ),
        check_vma=False,
    )
```

```python
import jax
import jax.numpy as jnp
from jax import lax
from jax.experimental import pallas as pl
from jax.experimental.pallas import tpu as pltpu
from jax.sharding import PartitionSpec as P

HQ = 8
HK = 2
HD = 128


tile_cols = 8
key_span = 14
negative_big = -1e30


def padded_2(cells, sides, width):
    for axis, dim in sides:
        count = lax.axis_size(axis)
        ends = count - 1
        head = lax.slice_in_dim(cells, 0, width, axis=dim)
        tail = lax.slice_in_dim(cells, cells.shape[dim] - width, cells.shape[dim], axis=dim)
        cells = jnp.concatenate(
            [
                lax.ppermute(tail, axis, [(i, (i + 1) % count) for i in range(ends)]),
                cells,
                lax.ppermute(head, axis, [((i + 1) % count, i) for i in range(ends)]),
            ],
            axis=dim,
        )
    return cells


def passed_along(value, axis, steps):
    count = lax.axis_size(axis)
    pairs = [(source, (source + steps) % count) for source in range(count)]
    return lax.ppermute(value, axis, pairs)


def to_tiles(block, group_size):
    band_rows = block.shape[0]
    count_tiles = block.shape[1] // tile_cols
    shaped = block.reshape(band_rows, count_tiles, tile_cols, HK, group_size, HD)
    shaped = shaped.transpose(1, 3, 4, 0, 2, 5)
    return shaped.reshape(count_tiles, HK, group_size, band_rows * tile_cols, HD)


def from_tiles(tiles, band_rows):
    count_tiles = tiles.shape[0]
    group_size = tiles.shape[2]
    shaped = tiles.reshape(count_tiles, HK, group_size, band_rows, tile_cols, HD)
    shaped = shaped.transpose(3, 0, 4, 1, 2, 5)
    return shaped.reshape(1, band_rows, count_tiles * tile_cols, HK * group_size * HD)


def to_windows(extended):
    ext_rows = extended.shape[1]
    total_width = extended.shape[2]
    padded = jnp.pad(extended, ((0, 0), (0, 0), (3, 3), (0, 0)))
    pieces = [
        padded[:, :, column_tile * tile_cols : column_tile * tile_cols + key_span]
        for column_tile in range(total_width // tile_cols)
    ]
    stacked = jnp.stack(pieces, 0)
    stacked = stacked.reshape(len(pieces), 2, ext_rows, key_span, HK, HD)
    stacked = stacked.transpose(1, 0, 4, 2, 3, 5)
    return stacked.reshape(2, len(pieces), HK, ext_rows * key_span, HD)


def from_windows(window_grads, ext_rows, total_width):
    count_tiles = window_grads.shape[1]
    shaped = window_grads.reshape(2, count_tiles, HK, ext_rows, key_span, HD)
    shaped = shaped.transpose(0, 1, 3, 4, 2, 5).reshape(2, count_tiles, ext_rows, key_span, HK * HD)
    summed = jnp.zeros((2, ext_rows, total_width + 6, HK * HD), jnp.float32)
    for column_tile in range(count_tiles):
        first_col = column_tile * tile_cols
        summed = summed.at[:, :, first_col : first_col + key_span].add(shaped[:, column_tile])
    return summed[:, :, 3 : 3 + total_width]


def spatial_live(offsets, band_rows, total_width):
    ext_rows = band_rows + 6
    count_tiles = total_width // tile_cols
    query_row = jnp.repeat(jnp.arange(band_rows), tile_cols)
    query_col = jnp.tile(jnp.arange(tile_cols), band_rows)
    key_row = jnp.repeat(jnp.arange(ext_rows), key_span)
    key_col = jnp.tile(jnp.arange(key_span), ext_rows)
    delta_row = key_row[None, :] - 3 - query_row[:, None]
    delta_col = key_col[None, :] - 3 - query_col[:, None]
    offset_hit = jnp.any(
        (delta_row[None] == offsets[:, 0, None, None])
        & (delta_col[None] == offsets[:, 1, None, None]),
        axis=0,
    )
    band_index = lax.axis_index("rows")
    image_rows = band_rows * lax.axis_size("rows")
    image_row = band_index * band_rows + key_row - 3
    row_inside = (image_row >= 0) & (image_row < image_rows)
    tile_first = jnp.arange(count_tiles) * tile_cols
    image_col = tile_first[:, None] + key_col[None, :] - 3
    col_inside = (image_col >= 0) & (image_col < total_width)
    return offset_hit[None] & row_inside[None, None] & col_inside[:, None, :]


def running_sum(entries):
    places = jnp.arange(entries.shape[0])
    return jnp.sum(jnp.where(places[None, :] <= places[:, None], entries[None, :], 0), axis=1)


def frame_allowed(frame_mask, clip_frames, distance):
    frames = lax.axis_size("tm")
    lags = min(4, frames)
    own_frame = lax.axis_index("tm")
    seen_frame = (own_frame - distance) % frames
    clip_ends = running_sum(clip_frames)
    clip_starts = clip_ends - clip_frames
    is_longest = (clip_frames == lags).astype(jnp.int32)
    first_longest = (is_longest == 1) & (running_sum(is_longest) == 1)
    rotation = jnp.sum(jnp.where(first_longest, clip_starts, 0))
    own_place = (own_frame + 2 + rotation) % frames
    seen_place = (seen_frame + 2 + rotation) % frames
    own_clip = jnp.sum((own_place >= clip_ends).astype(jnp.int32))
    seen_clip = jnp.sum((seen_place >= clip_ends).astype(jnp.int32))
    grid_rows = jnp.arange(frames)[:, None]
    grid_cols = jnp.arange(frames)[None, :]
    picked = jnp.sum(jnp.where((grid_rows == own_frame) & (grid_cols == seen_frame), frame_mask, 0))
    kept = (picked == 1) | (distance <= 1)
    return (own_clip == seen_clip) & (seen_place <= own_place) & kept


def fold_rims(extended_grads, band_rows):
    interior = extended_grads[:, 3 : 3 + band_rows]
    rim_rows = jnp.concatenate([extended_grads[:, :3], extended_grads[:, band_rows + 3 :]], 1)
    haloed = padded_2(rim_rows.astype(jnp.bfloat16), (("rows", 1),), 3).astype(rim_rows.dtype)
    interior = interior.at[:, :3].add(haloed[:, :3])
    return interior.at[:, band_rows - 3 :].add(haloed[:, 9:])


def body(queries, keys, values, grad_out, frame_mask, clip_frames, offsets):
    band_rows = queries.shape[1]
    total_width = queries.shape[2]
    ext_rows = band_rows + 6
    group_size = HQ // HK
    scale = HD ** (-0.5)
    lags = min(4, lax.axis_size("tm"))
    query_tiles = to_tiles(queries[0], group_size)
    grad_tiles = to_tiles(grad_out[0], group_size)
    spatial = spatial_live(offsets, band_rows, total_width)[:, None, None]
    allowed = [frame_allowed(frame_mask, clip_frames, distance) for distance in range(lags)]
    stacked = jnp.stack([keys[0], values[0]], 0)
    resident = padded_2(stacked, (("rows", 1),), 3)

    def pair_terms(extended):
        windows = to_windows(extended)
        logits = (
            jnp.einsum(
                "cgaqd,cgkd->cgaqk", query_tiles, windows[0], preferred_element_type=jnp.float32
            )
            * scale
        )
        grad_dot = jnp.einsum(
            "cgaqd,cgkd->cgaqk", grad_tiles, windows[1], preferred_element_type=jnp.float32
        )
        return (windows, logits, grad_dot)

    stat_shape = (total_width // tile_cols, HK, group_size, band_rows * tile_cols)
    running = (
        jnp.full(stat_shape, negative_big, jnp.float32),
        jnp.zeros(stat_shape, jnp.float32),
        jnp.zeros(stat_shape, jnp.float32),
    )
    visiting = resident
    visited = []
    for distance in range(lags):
        visited.append(visiting)
        extended = visiting
        live_mask = spatial & allowed[distance]
        run_max, run_sum, run_dot = running
        stat_windows, stat_logits, stat_grad_dot = pair_terms(extended)
        masked = jnp.where(live_mask, stat_logits, negative_big)
        new_max = jnp.maximum(run_max, jnp.max(masked, axis=-1))
        factor = jnp.exp(run_max - new_max)
        weights = jnp.where(live_mask, jnp.exp(stat_logits - new_max[..., None]), 0.0)
        running = (
            new_max,
            run_sum * factor + jnp.sum(weights, axis=-1),
            run_dot * factor + jnp.sum(weights * stat_grad_dot, axis=-1),
        )
        if distance + 1 < lags:
            visiting = passed_along(visiting, "tm", 1)
    log_total = running[0] + jnp.log(running[1])
    mean_grad = running[2] / running[1]
    query_total = jnp.zeros(stat_shape + (HD,), jnp.float32)
    carried = jnp.zeros(resident.shape, jnp.float32)
    visiting = resident
    for distance in range(lags):
        extended = visiting
        live_mask = spatial & allowed[distance]
        grad_windows, grad_logits, grad_grad_dot = pair_terms(extended)
        probs = jnp.where(live_mask, jnp.exp(grad_logits - log_total[..., None]), 0.0)
        probs_low = probs.astype(jnp.bfloat16)
        dscore = (probs * (grad_grad_dot - mean_grad[..., None])).astype(jnp.bfloat16)
        query_part = jnp.einsum(
            "cgaqk,cgkd->cgaqd", dscore, grad_windows[0], preferred_element_type=jnp.float32
        )
        key_part = (
            jnp.einsum("cgaqk,cgaqd->cgkd", dscore, query_tiles, preferred_element_type=jnp.float32)
            * scale
        )
        value_part = jnp.einsum(
            "cgaqk,cgaqd->cgkd", probs_low, grad_tiles, preferred_element_type=jnp.float32
        )
        query_part, window_grads = (query_part, jnp.stack([key_part, value_part], 0))
        query_total = query_total + query_part
        ext_grads = from_windows(window_grads, ext_rows, total_width)
        carried = carried + ext_grads
        if distance + 1 < lags:
            visiting = passed_along(visiting, "tm", 1)
            carried = passed_along(carried, "tm", 1)
    carried = passed_along(carried, "tm", 1 - lags)
    finished = fold_rims(carried, band_rows)
    grad_queries = from_tiles(query_total * scale, band_rows)
    return (grad_queries, finished[0][None], finished[1][None])


MESH = pl.DeviceIdType.MESH
LOG2E = 1.4426950408889634
SCALE = HD**-0.5
GROUP = HQ // HK


def lag_allowed(mask_ref, clip_ref, own_frame, frames, lag):
    clips = clip_ref.shape[0]
    seen_frame = lax.rem(own_frame - lag + frames, frames)
    total = jnp.int32(0)
    rotation = jnp.int32(0)
    found = jnp.int32(0)
    for clip in range(clips):
        length = clip_ref[clip]
        first = jnp.where(length == 4, 1, 0) * (1 - found)
        rotation = rotation + first * total
        found = found + first
        total = total + length
    own_place = own_frame + 2 + rotation
    own_place = jnp.where(own_place >= frames, own_place - frames, own_place)
    own_place = jnp.where(own_place >= frames, own_place - frames, own_place)
    seen_place = seen_frame + 2 + rotation
    seen_place = jnp.where(seen_place >= frames, seen_place - frames, seen_place)
    seen_place = jnp.where(seen_place >= frames, seen_place - frames, seen_place)
    own_clip = jnp.int32(0)
    seen_clip = jnp.int32(0)
    end = jnp.int32(0)
    for clip in range(clips):
        end = end + clip_ref[clip]
        own_clip = own_clip + jnp.where(own_place >= end, 1, 0)
        seen_clip = seen_clip + jnp.where(seen_place >= end, 1, 0)
    kept = jnp.maximum(jnp.where(mask_ref[own_frame, seen_frame] == 1, 1, 0), jnp.where(lag <= 1, 1, 0))
    same = jnp.where(own_clip == seen_clip, 1, 0)
    causal = jnp.where(seen_place <= own_place, 1, 0)
    return kept * same * causal


def fused(
    width, frames,
    mask_hbm, clip_hbm, offset_hbm, query_hbm, key_hbm, value_hbm, cot_hbm,
    dq_hbm, kv_grads_ref,
    dq_ref, mask_ref, clip_ref, offset_ref, query_ref, cot_ref, kv, grads, arrived, bias, probs, dots, tops, sums, means, dq_acc, load_sem, send_sem, recv_sem,
):
    tokens = query_ref.shape[0]
    heads_wide = HK * HD
    pairs = (
        (key_hbm, kv.at[0, :, pl.ds(0, heads_wide)]),
        (value_hbm, kv.at[0, :, pl.ds(heads_wide, heads_wide)]),
        (offset_hbm, offset_ref),
        (clip_hbm, clip_ref),
        (mask_hbm, mask_ref),
        (query_hbm, query_ref),
        (cot_hbm, cot_ref),
    )
    loads = [pltpu.make_async_copy(pair[0], pair[1], load_sem.at[i]) for i, pair in enumerate(pairs)]
    for load in loads[:2]:
        load.start()
    own = lax.axis_index("tm")
    core = lax.rem(own, 2)

    def device(step):
        return {"tm": lax.rem(own + step + frames, frames)}

    partner = device(1 - 2 * core)
    ahead, behind = device(2), device(frames - 2)
    far = device(jnp.where(core == 0, frames - 3, 3))
    second_to = device(jnp.where(core == 0, 1, 3))
    second_back = device(jnp.where(core == 0, frames - 3, frames - 1))

    barrier = pltpu.get_barrier_semaphore()
    for peer in (partner, ahead, behind, far):
        pl.semaphore_signal(barrier, inc=1, device_id=peer, device_id_type=MESH)
    for load in loads[:2]:
        load.wait()
    pl.semaphore_wait(barrier, 4)

    def remote(index, source, target, peer):
        return pltpu.make_async_remote_copy(
            src_ref=source, dst_ref=target, send_sem=send_sem.at[index], recv_sem=recv_sem.at[index],
            device_id=peer, device_id_type=MESH,
        )

    send_two = remote(0, kv.at[0], kv.at[2], ahead)
    send_one = remote(1, kv.at[0], kv.at[1], second_to)
    relay = remote(2, kv.at[2], kv.at[3], partner)
    send_two.start()
    for load in loads[2:]:
        load.start()
    for load in loads[2:]:
        load.wait()

    key_id = lax.broadcasted_iota(jnp.int32, (tokens, tokens), 0)
    query_id = lax.broadcasted_iota(jnp.int32, (tokens, tokens), 1)
    delta_col = lax.rem(key_id, width) - lax.rem(query_id, width)
    delta_row = key_id // width - query_id // width
    code = jnp.where((delta_col >= -3) & (delta_col <= 3), delta_row * 8 + delta_col, 1000)

    def mark(index, hit):
        wanted = offset_ref[0, index] * 8 + offset_ref[1, index]
        return jnp.where(code == wanted, 0.0, hit)

    bias[...] = lax.fori_loop(
        0, offset_ref.shape[1], mark, jnp.full((tokens, tokens), negative_big, jnp.float32), unroll=True
    )

    def lanes(index):
        return pl.ds(pl.multiple_of(index * HD, HD), HD)

    def scores(role, lag):
        allow = lag_allowed(mask_ref, clip_ref, own, frames, lag)
        shut = jnp.where(allow == 1, 0.0, negative_big).astype(jnp.float32)

        def head(h, _):
            group = h // GROUP
            key = kv[role, :, lanes(group)]
            value = kv[role, :, lanes(HK + group)]
            logit = lax.dot_general(
                key, query_ref[:, lanes(h)], (((1,), (1,)), ((), ())), preferred_element_type=jnp.float32
            )
            dot = lax.dot_general(
                value, cot_ref[:, lanes(h)], (((1,), (1,)), ((), ())), preferred_element_type=jnp.float32
            )
            logit = logit * (SCALE * LOG2E) + (bias[...] + shut)
            top = jnp.max(logit, axis=0, keepdims=True)
            weight = jnp.exp2(logit - top)
            probs[role, h] = weight
            dots[role, h] = dot
            tops[role, h] = top
            sums[role, h] = jnp.sum(weight, axis=0, keepdims=True)
            means[role, h] = jnp.sum(weight * dot, axis=0, keepdims=True)
            return 0

        lax.fori_loop(0, HQ, head, 0, unroll=4)

    lag_second = jnp.where(core == 0, 3, 1)
    lag_relay = jnp.where(core == 0, 1, 3)
    scores(0, jnp.int32(0))
    send_two.wait_send()
    send_one.start()
    send_two.wait_recv()
    relay.start()
    scores(2, jnp.int32(2))
    relay.wait_recv()
    scores(3, lag_relay)
    send_one.wait_recv()
    scores(1, lag_second)

    def finish(h, _):
        top = jnp.maximum(jnp.maximum(tops[0, h], tops[1, h]), jnp.maximum(tops[2, h], tops[3, h]))
        factors = [jnp.exp2(tops[role, h] - top) for role in range(4)]
        total = sum(factors[role] * sums[role, h] for role in range(4))
        dot = sum(factors[role] * means[role, h] for role in range(4))
        for role in range(4):
            tops[role, h] = factors[role] / total
        means[0, h] = dot / total
        return 0

    lax.fori_loop(0, HQ, finish, 0)

    def gradients(role, first, store):
        def one_group(group, _):
            key_turned = kv[role, :, lanes(group)].T
            key_sum = None
            value_sum = None
            for a in range(GROUP):
                h = group * GROUP + a
                prob = probs[role, h] * tops[role, h]
                score = (prob * (dots[role, h] - means[0, h])).astype(jnp.bfloat16)
                key_part = jnp.dot(score, query_ref[:, lanes(h)], preferred_element_type=jnp.float32)
                value_part = jnp.dot(
                    prob.astype(jnp.bfloat16), cot_ref[:, lanes(h)], preferred_element_type=jnp.float32
                )
                turned = jnp.dot(key_turned, score, preferred_element_type=jnp.float32)
                key_sum = key_part if a == 0 else key_sum + key_part
                value_sum = value_part if a == 0 else value_sum + value_part
                dq_acc[h] = turned if first else dq_acc[h] + turned
            store(group, key_sum * SCALE, value_sum)
            return 0

        lax.fori_loop(0, HK, one_group, 0)

    def store_out(role):
        def store(group, key_sum, value_sum):
            grads[role, :, lanes(group)] = key_sum.astype(jnp.bfloat16)
            grads[role, :, lanes(HK + group)] = value_sum.astype(jnp.bfloat16)

        return store

    back_relay = remote(3, grads.at[2], arrived.at[2], partner)
    back_two = remote(4, grads.at[1], arrived.at[1], behind)
    back_one = remote(5, grads.at[0], arrived.at[0], second_back)
    gradients(3, True, store_out(2))
    back_relay.start()
    gradients(1, False, store_out(0))
    back_one.start()

    def store_two(group, key_sum, value_sum):
        grads[1, :, lanes(group)] = key_sum.astype(jnp.bfloat16)
        grads[1, :, lanes(HK + group)] = value_sum.astype(jnp.bfloat16)

    gradients(2, False, store_two)
    back_relay.wait_recv()
    grads[1] = (grads[1].astype(jnp.float32) + arrived[2].astype(jnp.float32)).astype(jnp.bfloat16)
    back_two.start()

    def store_own(group, key_sum, value_sum):
        kv_grads_ref[0, :, lanes(group)] = key_sum
        kv_grads_ref[1, :, lanes(group)] = value_sum

    gradients(0, False, store_own)

    def query_out(h, _):
        dq_ref[:, lanes(h)] = dq_acc[h].T * SCALE
        return 0

    lax.fori_loop(0, HQ, query_out, 0, unroll=4)
    store_queries = pltpu.make_async_copy(dq_ref, dq_hbm, load_sem.at[7])
    store_queries.start()
    back_two.wait_recv()
    back_one.wait_recv()
    came = arrived[0].astype(jnp.float32) + arrived[1].astype(jnp.float32)
    kv_grads_ref[0] = kv_grads_ref[0] + came[:, :heads_wide]
    kv_grads_ref[1] = kv_grads_ref[1] + came[:, heads_wide:]
    for copy in (send_one, relay, back_relay, back_two, back_one):
        copy.wait_send()
    store_queries.wait()


def fused_body(queries, keys, values, grad_out, frame_mask, clip_frames, offsets):
    _, rows, width, wide = queries.shape
    tokens = rows * width
    narrow = keys.shape[3]
    frames = lax.axis_size("tm")

    def flat(array):
        return array.reshape(tokens, array.shape[3])

    hbm = pl.BlockSpec(memory_space=pltpu.HBM)
    vmem = pl.BlockSpec(memory_space=pltpu.VMEM)

    def kernel(*refs):
        fused(width, frames, *refs)

    dq, kv_grads = pl.pallas_call(
        kernel,
        out_shape=(
            jax.ShapeDtypeStruct((tokens, wide), jnp.float32),
            jax.ShapeDtypeStruct((2, tokens, narrow), jnp.float32),
        ),
        in_specs=[hbm] * 7,
        out_specs=(hbm, vmem),
        scratch_shapes=[
            pltpu.VMEM((tokens, wide), jnp.float32),
            pltpu.SMEM(frame_mask.shape, jnp.int32),
            pltpu.SMEM(clip_frames.shape, jnp.int32),
            pltpu.SMEM(offsets.shape[::-1], jnp.int32),
            pltpu.VMEM((tokens, wide), jnp.bfloat16),
            pltpu.VMEM((tokens, wide), jnp.bfloat16),
            pltpu.VMEM((4, tokens, 2 * narrow), jnp.bfloat16),
            pltpu.VMEM((3, tokens, 2 * narrow), jnp.bfloat16),
            pltpu.VMEM((3, tokens, 2 * narrow), jnp.bfloat16),
            pltpu.VMEM((tokens, tokens), jnp.float32),
            pltpu.VMEM((4, HQ, tokens, tokens), jnp.float32),
            pltpu.VMEM((4, HQ, tokens, tokens), jnp.float32),
            pltpu.VMEM((4, HQ, 1, tokens), jnp.float32),
            pltpu.VMEM((4, HQ, 1, tokens), jnp.float32),
            pltpu.VMEM((4, HQ, 1, tokens), jnp.float32),
            pltpu.VMEM((HQ, HD, tokens), jnp.float32),
            pltpu.SemaphoreType.DMA((8,)),
            pltpu.SemaphoreType.DMA((6,)),
            pltpu.SemaphoreType.DMA((6,)),
        ],
        compiler_params=pltpu.CompilerParams(
            collective_id=0, has_side_effects=True, vmem_limit_bytes=63 * 1024 * 1024 - 65536
        ),
    )(frame_mask, clip_frames, offsets.T, flat(queries), flat(keys), flat(values), flat(grad_out))
    shape = (1, rows, width)
    return dq.reshape(shape + (wide,)), kv_grads[0].reshape(shape + (narrow,)), kv_grads[1].reshape(shape + (narrow,))


def solution(mesh):
    whole_rows = mesh.shape["rows"] == 1 and mesh.shape["tm"] % 2 == 0 and mesh.shape["tm"] > 6
    return jax.shard_map(
        fused_body if whole_rows else body,
        mesh=mesh,
        in_specs=(
            P(("groups", "tm"), "rows", None, None),
            P(("groups", "tm"), "rows", None, None),
            P(("groups", "tm"), "rows", None, None),
            P(("groups", "tm"), "rows", None, None),
            P("groups", None),
            P("groups"),
            P(),
        ),
        out_specs=(
            P(("groups", "tm"), "rows", None, None),
            P(("groups", "tm"), "rows", None, None),
            P(("groups", "tm"), "rows", None, None),
        ),
        check_vma=False,
    )
```
